256 devices in a mesh: blk: 64 (over y_lo, x, z), dp: 4 (over y_hi, core).
Axes of the slice: x: 4, y: 4 (y_hi: 2, y_lo: 2; y = y_hi * 2 + y_lo), z: 8, core: 2. Of those that a mesh axis runs over, the one named last changes fastest.
Arguments:
- tokens: bfloat16 [4, 64, 2, 128, 1024], P('dp', 'blk'), may hold values from -11 to 11
- key_valid: int32 [4, 64, 2, 128], P('dp'), may hold values 0 or 1
- weights: bfloat16 [4096, 1024], replicated
- out_grad: bfloat16 [4, 64, 2, 128, 1024], P('dp', 'blk'), may hold values from -6 to 6
Outputs:
- grad_tokens: bfloat16 [4, 64, 2, 128, 1024], P('dp', 'blk')
- grad_out_weight: float32 [1024, 1024], P('blk', 'dp')
The draws below stay inside these ranges and needn't reach their ends.
All inputs are finite; a program needn't handle non-finite values. No bound on the sum of `key_valid` on one device may be relied on, other than what follows from the above.
Results may differ from the reference program's by a relative error of at most 0.024.
Values may be sent and summed in bfloat16 or wider, within the bound.
No kernel may reach another device: no remote copies, remote signals or barrier semaphores. Data moves between devices by JAX's collectives and lax.ppermute only.
A program may use at most 128 MiB of HBM per device.

```python
import jax
import jax.numpy as jnp
from jax import lax

HEADS = 16
HEAD_DIM = 64
D = 1024
WIN = 4
BLOCK = 128
SEQS = 1
SHOTS = 4
N_BLK = 64
N_DP = 4


def draw_tokens(key, part):
    key = jax.random.fold_in(key, 5)
    key_list = jax.random.split(key, 1)
    shape = (SEQS * N_DP, N_BLK, 2, BLOCK, D)
    values = jnp.clip(jax.random.normal(key_list[0], shape, jnp.float32), -5.0, 5.0)
    return values.astype(jnp.bfloat16)


def draw_weights(key, part):
    key = jax.random.fold_in(key, 11)
    key_list = jax.random.split(key, 1)
    inverse = D ** (-0.5)
    stacked = jnp.clip(jax.random.normal(key_list[0], (4 * D, D), jnp.float32), -5.0, 5.0)
    return (stacked * inverse).astype(jnp.bfloat16)


def with_ends(values, rng, low, high):
    longest = values.shape.index(max(values.shape))
    spots = []
    for shift in (0, 1):
        where = [jax.random.randint(jax.random.fold_in(rng, axis), (), 0, length) for axis, length in enumerate(values.shape)]
        where[longest] = (where[longest] + shift) % values.shape[longest]
        spots.append(tuple(where))
    return values.at[spots[0]].set(low).at[spots[1]].set(high)


def level_of(stream_key, extent, cuts, low, largest):
    gain = 1.0
    for position, blocks in cuts:
        heights = jax.random.uniform(jax.random.fold_in(jax.random.fold_in(stream_key, 6), position), (blocks,), jnp.float32, low / len(cuts), largest / len(cuts))
        gain = gain * jnp.repeat(jnp.exp(heights), extent[position] // blocks).reshape((-1,) + (1,) * (len(extent) - 1 - position))
    return gain


def bell_draw(own_key, shape, deviation, reach, cuts=(), held_as=jnp.bfloat16):
    entries = jax.random.normal(own_key, shape, jnp.float32) * deviation
    if len(cuts) > 0:
        entries = level_of(own_key, shape, cuts, -0.22, 0.18) * entries
    return jnp.clip(entries, min=-reach, max=reach).astype(held_as)


def setup_inputs(seed: int = 0) -> dict:
    key_of = jax.random.split(jax.random.key(seed), 5)
    tokens = draw_tokens(jax.random.fold_in(key_of[4], 71), 0)
    key_valid = with_ends((jax.random.randint(key_of[1], (SHOTS, N_BLK, 2, BLOCK), 0, 4) < 3).astype(jnp.int32), jax.random.fold_in(key_of[1], 1), 0, 1)
    weights = draw_weights(jax.random.fold_in(key_of[4], 71), 0)
    out_grad = bell_draw(key_of[3], (SHOTS, N_BLK, 2, BLOCK, D), 1.0, 6.0, ((0, 4), (1, 64)))
    return dict(tokens=tokens, key_valid=key_valid, weights=weights, out_grad=out_grad)


NEG_FILL = -1e30


def to_sequence(stored):
    return jnp.concatenate([stored[:, 0], jnp.flip(stored[:, 1], axis=0)], axis=0)


def to_stored(sequence):
    half_count = sequence.shape[0] // 2
    return jnp.stack([sequence[:half_count], jnp.flip(sequence[half_count:], axis=0)], axis=1)


def one_shot(shot_tokens, shot_valid, shot_grad, weights):
    model_width = shot_tokens.shape[-1]
    seq_length = 2 * N_BLK * BLOCK
    key_span = WIN * BLOCK
    margin = (WIN - 1) * BLOCK
    score_scale = HEAD_DIM ** -0.5
    contract = (((1,), (1,)), ((), ()))
    w_query = weights[:model_width]
    w_key = weights[model_width:2 * model_width]
    w_value = weights[2 * model_width:3 * model_width]
    w_out = weights[3 * model_width:]
    token_rows = to_sequence(shot_tokens).reshape(seq_length, model_width)
    grad_rows = to_sequence(shot_grad).reshape(seq_length, model_width)
    valid_rows = to_sequence(shot_valid).reshape(seq_length).astype(jnp.int32)
    queries = jnp.dot(token_rows, w_query, preferred_element_type=jnp.float32).astype(jnp.bfloat16)
    keyed = jnp.dot(token_rows, w_key, preferred_element_type=jnp.float32).astype(jnp.bfloat16)
    valued = jnp.dot(token_rows, w_value, preferred_element_type=jnp.float32).astype(jnp.bfloat16)
    d_attn = lax.dot_general(grad_rows, w_out, contract, preferred_element_type=jnp.float32).astype(jnp.bfloat16)
    key_pad = jnp.concatenate([jnp.zeros((margin, model_width), jnp.bfloat16), keyed], axis=0)
    value_pad = jnp.concatenate([jnp.zeros((margin, model_width), jnp.bfloat16), valued], axis=0)
    valid_pad = jnp.concatenate([jnp.zeros((margin,), jnp.int32), valid_rows], axis=0)

    def block_step(carry_pair, block_index):
        key_acc, value_acc = carry_pair
        first_row = block_index * BLOCK
        q_rows = lax.dynamic_slice_in_dim(queries, first_row, BLOCK, 0)
        do_rows = lax.dynamic_slice_in_dim(d_attn, first_row, BLOCK, 0)
        k_rows = lax.dynamic_slice_in_dim(key_pad, first_row, key_span, 0)
        v_rows = lax.dynamic_slice_in_dim(value_pad, first_row, key_span, 0)
        valid_keys = lax.dynamic_slice_in_dim(valid_pad, first_row, key_span, 0)
        q_pos = first_row + jnp.arange(BLOCK, dtype=jnp.int32)
        k_pos = first_row - margin + jnp.arange(key_span, dtype=jnp.int32)
        same_row = k_pos[None, :] == q_pos[:, None]
        allowed = (k_pos[None, :] >= 0) & (k_pos[None, :] <= q_pos[:, None]) & ((valid_keys[None, :] == 1) | same_row)
        q_heads = q_rows.reshape(BLOCK, HEADS, HEAD_DIM).astype(jnp.float32)
        k_heads = k_rows.reshape(key_span, HEADS, HEAD_DIM).astype(jnp.float32)
        v_heads = v_rows.reshape(key_span, HEADS, HEAD_DIM).astype(jnp.float32)
        do_heads = do_rows.reshape(BLOCK, HEADS, HEAD_DIM).astype(jnp.float32)
        scores = jnp.einsum('qhd,khd->hqk', q_heads, k_heads) * score_scale
        scores = jnp.where(allowed[None], scores, NEG_FILL)
        row_max = jnp.max(scores, axis=-1, keepdims=True)
        exp_terms = jnp.where(allowed[None], jnp.exp(scores - row_max), 0.0)
        probabilities = exp_terms / jnp.sum(exp_terms, axis=-1, keepdims=True)
        probs_low = lax.optimization_barrier(probabilities.astype(jnp.bfloat16)).astype(jnp.float32)
        out_rows = jnp.einsum('hqk,khd->qhd', probs_low, v_heads).reshape(BLOCK, model_width).astype(jnp.bfloat16)
        out_heads = lax.optimization_barrier(out_rows).reshape(BLOCK, HEADS, HEAD_DIM).astype(jnp.float32)
        delta_rows = jnp.einsum('qhd,qhd->hq', do_heads, out_heads)
        dprob = jnp.einsum('qhd,khd->hqk', do_heads, v_heads)
        dscore = (probabilities * (dprob - delta_rows[:, :, None])).astype(jnp.bfloat16)
        dscore = lax.optimization_barrier(dscore).astype(jnp.float32)
        grad_q = (jnp.einsum('hqk,khd->qhd', dscore, k_heads) * score_scale).reshape(BLOCK, model_width)
        grad_k = (jnp.einsum('hqk,qhd->khd', dscore, q_heads) * score_scale).reshape(key_span, model_width)
        grad_v = jnp.einsum('hqk,qhd->khd', probs_low, do_heads).reshape(key_span, model_width)
        key_acc = lax.dynamic_update_slice_in_dim(key_acc, lax.dynamic_slice_in_dim(key_acc, first_row, key_span, 0) + grad_k, first_row, 0)
        value_acc = lax.dynamic_update_slice_in_dim(value_acc, lax.dynamic_slice_in_dim(value_acc, first_row, key_span, 0) + grad_v, first_row, 0)
        return (key_acc, value_acc), (out_rows, grad_q)

    start_acc = jnp.zeros((seq_length + margin, model_width), jnp.float32)
    (key_acc, value_acc), (out_blocks, grad_q_blocks) = lax.scan(block_step, (start_acc, start_acc), jnp.arange(2 * N_BLK, dtype=jnp.int32))
    grad_q16 = grad_q_blocks.reshape(seq_length, model_width).astype(jnp.bfloat16)
    grad_k16 = key_acc[margin:].astype(jnp.bfloat16)
    grad_v16 = value_acc[margin:].astype(jnp.bfloat16)
    grad_in = lax.dot_general(grad_q16, w_query, contract, preferred_element_type=jnp.float32)
    grad_in = grad_in + lax.dot_general(grad_k16, w_key, contract, preferred_element_type=jnp.float32)
    grad_in = grad_in + lax.dot_general(grad_v16, w_value, contract, preferred_element_type=jnp.float32)
    grad_in = grad_in.astype(jnp.bfloat16).reshape(2 * N_BLK, BLOCK, model_width)
    out_all = out_blocks.reshape(seq_length, model_width)
    weight_term = lax.dot_general(out_all, grad_rows, (((0,), (0,)), ((), ())), preferred_element_type=jnp.float32)
    return to_stored(grad_in), weight_term


def reference(tokens, key_valid, weights, out_grad):
    def per_shot(shot_items):
        return one_shot(shot_items[0], shot_items[1], shot_items[2], weights)

    grad_blocks, weight_terms = lax.map(per_shot, (tokens, key_valid, out_grad))
    return grad_blocks, jnp.sum(weight_terms, axis=0)
```

```python
import jax
import jax.numpy as jnp
import numpy as np
from jax import lax
from jax.experimental import pallas as pl
from jax.experimental.pallas import tpu as pltpu
from jax.sharding import PartitionSpec as P

HEADS = 16
HEAD_DIM = 64
WIN = 4
BLOCK = 128
D = 1024
PAIR = 2 * HEAD_DIM
TILE = 256
BF = jnp.bfloat16
F32 = jnp.float32

BARRED = -1e30
FREE = 3e38
SCALE = HEAD_DIM**-0.5
EXP2_SCALE = float(SCALE * np.log2(np.e))

NN = (((1,), (0,)), ((), ()))
NT = (((1,), (1,)), ((), ()))


def mm(a, b, dims=NN):
    return lax.dot_general(a, b, dims, preferred_element_type=F32)


def params(mib):
    return pltpu.CompilerParams(vmem_limit_bytes=mib * 2**20)


def cost(flops, moved, exps=0):
    return pl.CostEstimate(flops=flops, bytes_accessed=moved, transcendentals=exps)


def weight_cols(which):
    return pl.BlockSpec((D, TILE), lambda t: (which, t))


def weight_rows(which):
    return pl.BlockSpec((TILE, D), lambda t: (which * (D // TILE) + t, 0))


def whole(shape):
    return pl.BlockSpec(shape, lambda t: (0,) * len(shape))


def own_kernel(x_ref, g_ref, wq_ref, wk_ref, wv_ref, wo_ref, q_ref, da_ref, kv_ref):
    x = x_ref[...].reshape(2 * BLOCK, D)
    g = g_ref[...].reshape(2 * BLOCK, D)
    q_ref[...] = mm(x, wq_ref[...]).astype(BF).reshape(2, BLOCK, TILE)
    da_ref[...] = mm(g, wo_ref[...], NT).astype(BF).reshape(2, BLOCK, TILE)
    kv_ref[0] = mm(x, wk_ref[...]).astype(BF).reshape(2, BLOCK, TILE)
    kv_ref[1] = mm(x, wv_ref[...]).astype(BF).reshape(2, BLOCK, TILE)


def own_projections(x, g, weights):
    rows = jax.ShapeDtypeStruct((2, BLOCK, D), BF)
    row_tile = pl.BlockSpec((2, BLOCK, TILE), lambda t: (0, 0, t))
    return pl.pallas_call(
        own_kernel,
        grid=(D // TILE,),
        in_specs=[
            whole((2, BLOCK, D)),
            whole((2, BLOCK, D)),
            weight_cols(0),
            weight_cols(1),
            weight_cols(2),
            weight_rows(3),
        ],
        out_specs=[row_tile, row_tile, pl.BlockSpec((2, 2, BLOCK, TILE), lambda t: (0, 0, 0, t))],
        out_shape=[rows, rows, jax.ShapeDtypeStruct((2, 2, BLOCK, D), BF)],
        compiler_params=params(32),
        cost_estimate=cost(8 * 2 * BLOCK * D * D, 8 * D * D + 12 * BLOCK * D),
        name="own_projections",
    )(x, g, weights, weights, weights, weights)


def halo_kernel(up_ref, down_ref, wk_ref, wv_ref, kv_ref):
    x = jnp.concatenate([up_ref[...], down_ref[...]], axis=0)
    kv_ref[0] = mm(x, wk_ref[...]).astype(BF).reshape(2, BLOCK, TILE)
    kv_ref[1] = mm(x, wv_ref[...]).astype(BF).reshape(2, BLOCK, TILE)


def halo_projections(up, down, weights):
    return pl.pallas_call(
        halo_kernel,
        grid=(D // TILE,),
        in_specs=[whole((BLOCK, D)), whole((BLOCK, D)), weight_cols(1), weight_cols(2)],
        out_specs=pl.BlockSpec((2, 2, BLOCK, TILE), lambda t: (0, 0, 0, t)),
        out_shape=jax.ShapeDtypeStruct((2, 2, BLOCK, D), BF),
        compiler_params=params(32),
        cost_estimate=cost(4 * 2 * BLOCK * D * D, 4 * D * D + 12 * BLOCK * D),
        name="halo_projections",
    )(up, down, weights, weights)


def attention_kernel(
    q_ref, da_ref, kv3_ref, kv2_ref, kv1_ref, kv0_ref, bias_ref,
    out_ref, dq_ref, d3_ref, d2_ref, d1_ref, d0_ref,
):
    lane = lax.broadcasted_iota(jnp.int32, (BLOCK, PAIR), 1)
    first = lane < HEAD_DIM

    def split(rows):
        zero = jnp.zeros_like(rows)
        return jnp.concatenate([jnp.where(first, rows, zero), jnp.where(first, zero, rows)], axis=0)

    def own_heads(square):
        return jnp.concatenate([square[:HEAD_DIM, :BLOCK], square[HEAD_DIM:, BLOCK:]], axis=0)

    kv_refs = (kv3_ref, kv2_ref, kv1_ref, kv0_ref)
    keys = jnp.concatenate([ref[0, 0] for ref in kv_refs], axis=0)
    values = jnp.concatenate([ref[1, 0] for ref in kv_refs], axis=0)
    d_attn = da_ref[0]
    q_split = split(q_ref[0])
    da_split = split(d_attn)
    bias = bias_ref[0]
    scores = jnp.minimum(mm(keys, q_split, NT), jnp.concatenate([bias, bias], axis=1))
    top = jnp.max(scores, axis=0, keepdims=True)
    terms = jnp.exp2((scores - top) * EXP2_SCALE)
    probs = terms * (1.0 / jnp.sum(terms, axis=0, keepdims=True))
    probs_low = probs.astype(BF)
    out_t = own_heads(mm(values.T, probs_low)).astype(BF)
    out_ref[0] = out_t.T
    weighted = d_attn.T.astype(F32) * out_t.astype(F32)
    delta = jnp.concatenate(
        [
            jnp.sum(weighted[:HEAD_DIM], axis=0, keepdims=True),
            jnp.sum(weighted[HEAD_DIM:], axis=0, keepdims=True),
        ],
        axis=1,
    )
    dscore = (probs * (mm(values, da_split, NT) - delta)).astype(BF)
    dq_ref[0] = (own_heads(mm(keys.T, dscore)) * SCALE).astype(BF).T
    d_keys = (mm(dscore, q_split) * SCALE).astype(BF)
    d_values = mm(probs_low, da_split).astype(BF)
    for place, ref in enumerate((d3_ref, d2_ref, d1_ref, d0_ref)):
        ref[0, 0] = d_keys[place * BLOCK : (place + 1) * BLOCK]
        ref[1, 0] = d_values[place * BLOCK : (place + 1) * BLOCK]


def attention(q, da, kvs, bias):
    rows = jax.ShapeDtypeStruct((2, BLOCK, D), BF)
    pairs = jax.ShapeDtypeStruct((2, 2, BLOCK, D), BF)
    row_spec = pl.BlockSpec((1, BLOCK, PAIR), lambda h, p: (h, 0, p))
    pair_spec = pl.BlockSpec((2, 1, BLOCK, PAIR), lambda h, p: (0, h, 0, p))
    bias_spec = pl.BlockSpec((1, WIN * BLOCK, BLOCK), lambda h, p: (h, 0, 0))
    return pl.pallas_call(
        attention_kernel,
        grid=(2, HEADS // 2),
        in_specs=[row_spec, row_spec] + [pair_spec] * 4 + [bias_spec],
        out_specs=[row_spec, row_spec] + [pair_spec] * 4,
        out_shape=[rows, rows] + [pairs] * 4,
        compiler_params=params(32),
        cost_estimate=cost(2 * 10 * BLOCK * WIN * BLOCK * D * 4, 12 * 2**20, 2**21),
        name="attention",
    )(q, da, *kvs, bias)


def back_kernel(d_ref, wk_ref, wv_ref, out_ref):
    rows = mm(d_ref[0].reshape(2 * BLOCK, D), wk_ref[...], NT)
    rows += mm(d_ref[1].reshape(2 * BLOCK, D), wv_ref[...], NT)
    out_ref[...] = rows.reshape(2, BLOCK, TILE).astype(out_ref.dtype)


def back_projections(d, weights, dtype):
    return pl.pallas_call(
        back_kernel,
        grid=(D // TILE,),
        in_specs=[whole((2, 2, BLOCK, D)), weight_rows(1), weight_rows(2)],
        out_specs=pl.BlockSpec((2, BLOCK, TILE), lambda t: (0, 0, t)),
        out_shape=jax.ShapeDtypeStruct((2, BLOCK, D), dtype),
        compiler_params=params(32),
        cost_estimate=cost(4 * 2 * BLOCK * D * D, 4 * D * D + 12 * BLOCK * D),
        name="back_projections",
    )(d, weights, weights)


def last_kernel(d_ref, dq_ref, wq_ref, wk_ref, wv_ref, out_ref):
    rows = mm(dq_ref[...].reshape(2 * BLOCK, D), wq_ref[...], NT)
    rows += mm(d_ref[0].reshape(2 * BLOCK, D), wk_ref[...], NT)
    rows += mm(d_ref[1].reshape(2 * BLOCK, D), wv_ref[...], NT)
    out_ref[...] = rows.reshape(2, BLOCK, TILE)


def last_projections(d, dq, weights):
    return pl.pallas_call(
        last_kernel,
        grid=(D // TILE,),
        in_specs=[
            whole((2, 2, BLOCK, D)),
            whole((2, BLOCK, D)),
            weight_rows(0),
            weight_rows(1),
            weight_rows(2),
        ],
        out_specs=pl.BlockSpec((2, BLOCK, TILE), lambda t: (0, 0, t)),
        out_shape=jax.ShapeDtypeStruct((2, BLOCK, D), F32),
        compiler_params=params(32),
        cost_estimate=cost(6 * 2 * BLOCK * D * D, 6 * D * D + 16 * BLOCK * D),
        name="last_projections",
    )(d, dq, weights, weights, weights)


def outer_kernel(core_ref, o_ref, keep_ref, send_ref, kept_ref, sent_ref):
    o_t = o_ref[...].reshape(2 * BLOCK, D).T
    for g_ref, r_ref in ((send_ref, sent_ref), (keep_ref, kept_ref)):
        product = mm(o_t, g_ref[...].reshape(2 * BLOCK, TILE)).astype(BF)
        r_ref[0, 0] = product[:, :BLOCK]
        r_ref[0, 1] = product[:, BLOCK:]


def outer_products(o, g, core):
    result = jax.ShapeDtypeStruct((2, 2, D, BLOCK), BF)
    result_spec = pl.BlockSpec((1, 2, D, BLOCK), lambda y, c: (y, 0, 0, 0))
    return pl.pallas_call(
        outer_kernel,
        grid_spec=pltpu.PrefetchScalarGridSpec(
            num_scalar_prefetch=1,
            grid=(2,),
            in_specs=[
                pl.BlockSpec((2, BLOCK, D), lambda y, c: (0, 0, 0)),
                pl.BlockSpec((2, BLOCK, TILE), lambda y, c: (0, 0, 2 * y + c[0])),
                pl.BlockSpec((2, BLOCK, TILE), lambda y, c: (0, 0, 2 * y + 1 - c[0])),
            ],
            out_specs=[result_spec, result_spec],
        ),
        out_shape=[result, result],
        compiler_params=params(32),
        cost_estimate=cost(4 * BLOCK * D * D, 2 * D * D + 8 * BLOCK * D),
        name="outer_products",
    )(core.reshape(1), o, g, g)


def chip_pairs(move):
    pairs = []
    for y in range(4):
        for x in range(4):
            for z in range(8):
                y2, x2, z2 = move(y, x, z)
                for core in range(2):
                    pairs.append((place(y, x, z, core), place(y2, x2, z2, core)))
    return pairs


def place(y, x, z, core):
    return ((y % 2) * 32 + x * 8 + z) * 4 + (y // 2) * 2 + core


FLIP = ((1, 0, 3, 2), (3, 2, 1, 0))


def add(a, b):
    return (a.astype(F32) + b.astype(F32)).astype(BF)


def ring_first(v, dim, index, pairs):
    def pick(i):
        return lax.slice_in_dim(v, i, i + 1, axis=dim)

    outer = jnp.concatenate([pick(0), pick(3)], axis=dim)
    inner = lax.slice_in_dim(v, 1, 3, axis=dim)
    mine = (index == 0) | (index == 3)
    moved = lax.ppermute(jnp.where(mine, inner, outer), ("blk", "dp"), pairs)
    return add(jnp.where(mine, outer, inner), moved)


def halve(v, dim, bit, pairs):
    low = lax.slice_in_dim(v, 0, 1, axis=dim)
    high = lax.slice_in_dim(v, 1, 2, axis=dim)
    moved = lax.ppermute(jnp.where(bit == 0, high, low), ("blk", "dp"), pairs)
    return add(jnp.where(bit == 0, low, high), moved)


def reduce_outer(kept, sent, y, x, z):
    core_pairs = [(i, i ^ 1) for i in range(4)]
    total = add(kept, lax.ppermute(sent, "dp", core_pairs))
    total = total.reshape(2, 2, 2, 4, 8, 16, BLOCK)
    parts = [total[:, i].reshape(4, 4, 8, 16, BLOCK) for i in range(2)]
    rings = (
        (0, y, [chip_pairs(lambda a, b, c, f=f: (f[a], b, c)) for f in FLIP]),
        (1, x, [chip_pairs(lambda a, b, c, f=f: (a, f[b], c)) for f in FLIP]),
    )
    for turn in range(2):
        dim_of = [rings[(i + turn + 1) % 2] for i in range(2)]
        parts = [ring_first(v, d, i, m[0]) for v, (d, i, m) in zip(parts, dim_of)]
        parts = [halve(v, d, i // 2, m[1]) for v, (d, i, m) in zip(parts, dim_of)]
    v = jnp.concatenate(parts, axis=0).reshape(2, 2, 2, 2, 16, BLOCK)
    for k, dim in ((1, 3), (2, 2), (4, 1)):
        v = halve(v, dim, (z // k) % 2, chip_pairs(lambda a, b, c, k=k: (a, b, c ^ k)))
    v = v.reshape(2, 16, BLOCK)
    return jnp.concatenate([v[0], v[1]], axis=1).astype(F32)


def score_limits(key_valid, position):
    blocks = 2 * 64
    both = jnp.stack([position, blocks - 1 - position])
    seq_valid = jnp.concatenate([key_valid[0, :, 0], jnp.flip(key_valid[0, :, 1], axis=0)], axis=0)
    seq_valid = jnp.concatenate([jnp.zeros((WIN - 1, BLOCK), jnp.int32), seq_valid], axis=0)
    valid = jnp.stack(
        [lax.dynamic_slice_in_dim(seq_valid, both[i], WIN, 0).reshape(WIN * BLOCK) for i in range(2)]
    )
    q_pos = jnp.arange(BLOCK, dtype=jnp.int32)[None, None, :]
    k_pos = (jnp.arange(WIN * BLOCK, dtype=jnp.int32) - (WIN - 1) * BLOCK)[None, :, None]
    inside = k_pos + both[:, None, None] * BLOCK >= 0
    allowed = inside & (k_pos <= q_pos) & ((valid[:, :, None] == 1) | (k_pos == q_pos))
    return jnp.where(allowed, FREE, BARRED).astype(F32)


def per_device(tokens, key_valid, weights, out_grad):
    position = lax.axis_index("blk")
    shot = lax.axis_index("dp")
    at_last = position == 63
    up = [(i, i + 1) for i in range(63)]
    down = [(i + 1, i) for i in range(63)]
    x = tokens.reshape(2, BLOCK, D)
    g = out_grad.reshape(2, BLOCK, D)

    bias = score_limits(key_valid, position)
    q, da, kv0 = own_projections(x, g, weights)
    kvs = [kv0]
    state_up, state_down = x[0], x[1]
    for _ in range(WIN - 1):
        new_up = lax.ppermute(state_up, "blk", up)
        new_down = jnp.where(at_last, state_up, lax.ppermute(state_down, "blk", down))
        kvs.append(halo_projections(new_up, new_down, weights))
        state_up, state_down = new_up, new_down
    o, dq, d3, d2, d1, d0 = attention(q, da, kvs[::-1], bias)

    kept, sent = outer_products(o, g, shot % 2)
    w_grad = reduce_outer(kept, sent, (shot // 2) * 2 + position // 32, (position // 8) % 4, position % 8)

    returned = back_projections(d3, weights, BF)
    terms = [back_projections(d2, weights, BF), back_projections(d1, weights, BF), last_projections(d0, dq, weights)]
    for term in terms:
        from_after = lax.ppermute(returned[0], "blk", down)
        from_before = lax.ppermute(returned[1], "blk", up)
        extra = jnp.where(at_last, returned[1], jnp.zeros_like(returned[1])).astype(F32)
        total = jnp.stack(
            [term[0].astype(F32) + from_after.astype(F32) + extra, term[1].astype(F32) + from_before.astype(F32)]
        )
        returned = total.astype(BF)
    return returned.reshape(tokens.shape), w_grad


def solution(mesh):
    placed = (
        P("dp", "blk", None, None, None),
        P("dp", None, None, None),
        P(),
        P("dp", "blk", None, None, None),
    )
    return jax.shard_map(
        per_device,
        mesh=mesh,
        in_specs=placed,
        out_specs=(P("dp", "blk", None, None, None), P("blk", "dp")),
        check_vma=False,
    )
```

```python
import jax
import jax.numpy as jnp
import numpy as np
from jax import lax
from jax.experimental import pallas as pl
from jax.experimental.pallas import tpu as pltpu
from jax.sharding import PartitionSpec as P

HEADS = 16
HEAD_DIM = 64
WIN = 4
BLOCK = 128
D = 1024
PAIR = 2 * HEAD_DIM
PAIRS_A_STEP = 4
TILE = 256
BF = jnp.bfloat16
F32 = jnp.float32

BARRED = -1e30
FREE = 3e38
SCALE = HEAD_DIM**-0.5
EXP2_SCALE = float(SCALE * np.log2(np.e))

NN = (((1,), (0,)), ((), ()))
NT = (((1,), (1,)), ((), ()))


def mm(a, b, dims=NN):
    return lax.dot_general(a, b, dims, preferred_element_type=F32)


def params(mib):
    return pltpu.CompilerParams(vmem_limit_bytes=mib * 2**20)


def cost(flops, moved, exps=0):
    return pl.CostEstimate(flops=flops, bytes_accessed=moved, transcendentals=exps)


def weight_cols(which):
    return pl.BlockSpec((D, TILE), lambda t: (which, t))


def weight_rows(which):
    return pl.BlockSpec((TILE, D), lambda t: (which * (D // TILE) + t, 0))


def whole(shape):
    return pl.BlockSpec(shape, lambda t: (0,) * len(shape))


def own_kernel(x_ref, g_ref, wq_ref, wk_ref, wv_ref, wo_ref, q_ref, da_ref, kv_ref):
    x = x_ref[...].reshape(2 * BLOCK, D)
    g = g_ref[...].reshape(2 * BLOCK, D)
    q_ref[...] = mm(x, wq_ref[...]).astype(BF).reshape(2, BLOCK, TILE)
    da_ref[...] = mm(g, wo_ref[...], NT).astype(BF).reshape(2, BLOCK, TILE)
    kv_ref[0] = mm(x, wk_ref[...]).astype(BF).reshape(2, BLOCK, TILE)
    kv_ref[1] = mm(x, wv_ref[...]).astype(BF).reshape(2, BLOCK, TILE)


def own_projections(x, g, weights):
    rows = jax.ShapeDtypeStruct((2, BLOCK, D), BF)
    row_tile = pl.BlockSpec((2, BLOCK, TILE), lambda t: (0, 0, t))
    return pl.pallas_call(
        own_kernel,
        grid=(D // TILE,),
        in_specs=[
            whole((2, BLOCK, D)),
            whole((2, BLOCK, D)),
            weight_cols(0),
            weight_cols(1),
            weight_cols(2),
            weight_rows(3),
        ],
        out_specs=[row_tile, row_tile, pl.BlockSpec((2, 2, BLOCK, TILE), lambda t: (0, 0, 0, t))],
        out_shape=[rows, rows, jax.ShapeDtypeStruct((2, 2, BLOCK, D), BF)],
        compiler_params=params(32),
        cost_estimate=cost(8 * 2 * BLOCK * D * D, 8 * D * D + 12 * BLOCK * D),
        name="own_projections",
    )(x, g, weights, weights, weights, weights)


def halo_kernel(up_ref, down_ref, wk_ref, wv_ref, kv_ref):
    x = jnp.concatenate([up_ref[...], down_ref[...]], axis=0)
    kv_ref[0] = mm(x, wk_ref[...]).astype(BF).reshape(2, BLOCK, TILE)
    kv_ref[1] = mm(x, wv_ref[...]).astype(BF).reshape(2, BLOCK, TILE)


def halo_projections(up, down, weights):
    return pl.pallas_call(
        halo_kernel,
        grid=(D // TILE,),
        in_specs=[whole((BLOCK, D)), whole((BLOCK, D)), weight_cols(1), weight_cols(2)],
        out_specs=pl.BlockSpec((2, 2, BLOCK, TILE), lambda t: (0, 0, 0, t)),
        out_shape=jax.ShapeDtypeStruct((2, 2, BLOCK, D), BF),
        compiler_params=params(32),
        cost_estimate=cost(4 * 2 * BLOCK * D * D, 4 * D * D + 12 * BLOCK * D),
        name="halo_projections",
    )(up, down, weights, weights)


def attention_kernel(
    q_ref, da_ref, kv3_ref, kv2_ref, kv1_ref, kv0_ref, bias_ref,
    out_ref, dq_ref, d3_ref, d2_ref, d1_ref, d0_ref,
):
    first = lax.broadcasted_iota(jnp.int32, (BLOCK, PAIR), 1) < HEAD_DIM
    kv_refs = (kv3_ref, kv2_ref, kv1_ref, kv0_ref)
    d_refs = (d3_ref, d2_ref, d1_ref, d0_ref)
    lanes = [slice(i * PAIR, (i + 1) * PAIR) for i in range(PAIRS_A_STEP)]

    def split(rows):
        zero = jnp.zeros_like(rows)
        return jnp.concatenate([jnp.where(first, rows, zero), jnp.where(first, zero, rows)], axis=0)

    def merge(rows):
        return jnp.where(first, rows[:BLOCK], rows[BLOCK:])

    def twice(rows):
        return jnp.concatenate([rows, rows], axis=0)

    bias = twice(bias_ref[0])
    ones = jnp.ones((WIN * BLOCK, PAIR), BF)
    keys = [jnp.concatenate([ref[0, 0, :, c] for ref in kv_refs], axis=0) for c in lanes]
    values = [jnp.concatenate([ref[1, 0, :, c] for ref in kv_refs], axis=0) for c in lanes]
    queries = [split(q_ref[0, :, c]) for c in lanes]
    d_attn = [split(da_ref[0, :, c]) for c in lanes]
    scores = [jnp.minimum(mm(q, k, NT), bias) for q, k in zip(queries, keys)]
    tops = [jnp.max(s, axis=1, keepdims=True) for s in scores]
    terms = [jnp.exp2((s - t) * EXP2_SCALE).astype(BF) for s, t in zip(scores, tops)]
    sums = [mm(t, jnp.concatenate([v, ones], axis=1)) for t, v in zip(terms, values)]
    shares = [1.0 / s[:, PAIR:] for s in sums]
    outs = [merge(s[:, :PAIR] * r).astype(BF) for s, r in zip(sums, shares)]
    for c, o in zip(lanes, outs):
        out_ref[0, :, c] = o
    scaled = [d.astype(F32) * r for d, r in zip(d_attn, shares)]
    deltas = [
        jnp.sum(d * twice(o.astype(F32)), axis=1, keepdims=True) for d, o in zip(scaled, outs)
    ]
    scaled = [d.astype(BF) for d in scaled]
    d_probs = [mm(d, v, NT) for d, v in zip(scaled, values)]
    d_scores = [(p - d).astype(BF) * t for p, d, t in zip(d_probs, deltas, terms)]
    d_values = [mm(d.T, t).astype(BF).T for d, t in zip(scaled, terms)]
    d_queries = [merge(mm(d, k)) for d, k in zip(d_scores, keys)]
    for c, d in zip(lanes, d_queries):
        dq_ref[0, :, c] = (d * SCALE).astype(BF)
    d_keys = [(mm(q.T, d) * SCALE).astype(BF).T for q, d in zip(queries, d_scores)]
    for c, dk, dv in zip(lanes, d_keys, d_values):
        for i, ref in enumerate(d_refs):
            ref[0, 0, :, c] = dk[i * BLOCK : (i + 1) * BLOCK]
            ref[1, 0, :, c] = dv[i * BLOCK : (i + 1) * BLOCK]


def attention(q, da, kvs, bias):
    rows = jax.ShapeDtypeStruct((2, BLOCK, D), BF)
    pairs = jax.ShapeDtypeStruct((2, 2, BLOCK, D), BF)
    width = PAIRS_A_STEP * PAIR
    row_spec = pl.BlockSpec((1, BLOCK, width), lambda h, p: (h, 0, p))
    pair_spec = pl.BlockSpec((2, 1, BLOCK, width), lambda h, p: (0, h, 0, p))
    bias_spec = pl.BlockSpec((1, BLOCK, WIN * BLOCK), lambda h, p: (h, 0, 0))
    return pl.pallas_call(
        attention_kernel,
        grid=(2, D // width),
        in_specs=[row_spec, row_spec] + [pair_spec] * 4 + [bias_spec],
        out_specs=[row_spec, row_spec] + [pair_spec] * 4,
        out_shape=[rows, rows] + [pairs] * 4,
        compiler_params=params(32),
        cost_estimate=cost(2 * 10 * BLOCK * WIN * BLOCK * D * 2, 12 * 2**20, 2**21),
        name="attention",
    )(q, da, *kvs, bias)


def back_kernel(d_ref, wk_ref, wv_ref, out_ref):
    rows = mm(d_ref[0].reshape(2 * BLOCK, D), wk_ref[...], NT)
    rows += mm(d_ref[1].reshape(2 * BLOCK, D), wv_ref[...], NT)
    out_ref[...] = rows.reshape(2, BLOCK, TILE).astype(out_ref.dtype)


def back_projections(d, weights, dtype):
    return pl.pallas_call(
        back_kernel,
        grid=(D // TILE,),
        in_specs=[whole((2, 2, BLOCK, D)), weight_rows(1), weight_rows(2)],
        out_specs=pl.BlockSpec((2, BLOCK, TILE), lambda t: (0, 0, t)),
        out_shape=jax.ShapeDtypeStruct((2, BLOCK, D), dtype),
        compiler_params=params(32),
        cost_estimate=cost(4 * 2 * BLOCK * D * D, 4 * D * D + 12 * BLOCK * D),
        name="back_projections",
    )(d, weights, weights)


def last_kernel(d_ref, dq_ref, wq_ref, wk_ref, wv_ref, out_ref):
    rows = mm(dq_ref[...].reshape(2 * BLOCK, D), wq_ref[...], NT)
    rows += mm(d_ref[0].reshape(2 * BLOCK, D), wk_ref[...], NT)
    rows += mm(d_ref[1].reshape(2 * BLOCK, D), wv_ref[...], NT)
    out_ref[...] = rows.reshape(2, BLOCK, TILE)


def last_projections(d, dq, weights):
    return pl.pallas_call(
        last_kernel,
        grid=(D // TILE,),
        in_specs=[
            whole((2, 2, BLOCK, D)),
            whole((2, BLOCK, D)),
            weight_rows(0),
            weight_rows(1),
            weight_rows(2),
        ],
        out_specs=pl.BlockSpec((2, BLOCK, TILE), lambda t: (0, 0, t)),
        out_shape=jax.ShapeDtypeStruct((2, BLOCK, D), F32),
        compiler_params=params(32),
        cost_estimate=cost(6 * 2 * BLOCK * D * D, 6 * D * D + 16 * BLOCK * D),
        name="last_projections",
    )(d, dq, weights, weights, weights)


def outer_kernel(core_ref, o_ref, keep_ref, send_ref, kept_ref, sent_ref):
    o_t = o_ref[...].reshape(2 * BLOCK, D).T
    for g_ref, r_ref in ((send_ref, sent_ref), (keep_ref, kept_ref)):
        r_ref[0] = mm(o_t, g_ref[...].reshape(2 * BLOCK, TILE)).astype(BF)


def outer_products(o, g, core):
    result = jax.ShapeDtypeStruct((2, D, TILE), BF)
    result_spec = pl.BlockSpec((1, D, TILE), lambda y, c: (y, 0, 0))
    return pl.pallas_call(
        outer_kernel,
        grid_spec=pltpu.PrefetchScalarGridSpec(
            num_scalar_prefetch=1,
            grid=(2,),
            in_specs=[
                pl.BlockSpec((2, BLOCK, D), lambda y, c: (0, 0, 0)),
                pl.BlockSpec((2, BLOCK, TILE), lambda y, c: (0, 0, 2 * y + c[0])),
                pl.BlockSpec((2, BLOCK, TILE), lambda y, c: (0, 0, 2 * y + 1 - c[0])),
            ],
            out_specs=[result_spec, result_spec],
        ),
        out_shape=[result, result],
        compiler_params=params(32),
        cost_estimate=cost(4 * BLOCK * D * D, 2 * D * D + 8 * BLOCK * D),
        name="outer_products",
    )(core.reshape(1), o, g, g)


def place(y, x, z, core):
    return ((y % 2) * 32 + x * 8 + z) * 4 + (y // 2) * 2 + core


CORE_PAIRS = [(i, i ^ 1) for i in range(4)]
PLANES = [
    [place(y, x, z, core) for y in range(4) for x in range(4)] for z in range(8) for core in range(2)
]
LINES = [[32 * y + 8 * x + z for z in range(8)] for y in range(2) for x in range(4)]


def add(a, b):
    return (a.astype(F32) + b.astype(F32)).astype(BF)


def reduce_outer(kept, sent):
    total = add(kept, lax.ppermute(sent, "dp", CORE_PAIRS))
    total = total.reshape(16, 8 * 16, TILE)
    total = lax.all_to_all(total, ("blk", "dp"), 0, 0, axis_index_groups=PLANES)
    total = jnp.sum(total.astype(F32), axis=0).astype(BF).reshape(8, 16, TILE)
    total = lax.all_to_all(total, "blk", 0, 0, axis_index_groups=LINES)
    return jnp.sum(total.astype(F32), axis=0)


def score_limits(key_valid, position):
    blocks = 2 * 64
    both = jnp.stack([position, blocks - 1 - position])
    seq_valid = jnp.concatenate([key_valid[0, :, 0], jnp.flip(key_valid[0, :, 1], axis=0)], axis=0)
    seq_valid = jnp.concatenate([jnp.zeros((WIN - 1, BLOCK), jnp.int32), seq_valid], axis=0)
    valid = jnp.stack(
        [lax.dynamic_slice_in_dim(seq_valid, both[i], WIN, 0).reshape(WIN * BLOCK) for i in range(2)]
    )
    q_pos = jnp.arange(BLOCK, dtype=jnp.int32)[None, :, None]
    k_pos = (jnp.arange(WIN * BLOCK, dtype=jnp.int32) - (WIN - 1) * BLOCK)[None, None, :]
    inside = k_pos + both[:, None, None] * BLOCK >= 0
    allowed = inside & (k_pos <= q_pos) & ((valid[:, None, :] == 1) | (k_pos == q_pos))
    return jnp.where(allowed, FREE, BARRED).astype(F32)


def per_device(tokens, key_valid, weights, out_grad):
    position = lax.axis_index("blk")
    shot = lax.axis_index("dp")
    at_last = position == 63
    up = [(i, i + 1) for i in range(63)]
    down = [(i + 1, i) for i in range(63)]
    x = tokens.reshape(2, BLOCK, D)
    g = out_grad.reshape(2, BLOCK, D)

    bias = score_limits(key_valid, position)
    q, da, kv0 = own_projections(x, g, weights)
    kvs = [kv0]
    state_up, state_down = x[0], x[1]
    for _ in range(WIN - 1):
        new_up = lax.ppermute(state_up, "blk", up)
        new_down = jnp.where(at_last, state_up, lax.ppermute(state_down, "blk", down))
        new_up, new_down, kvs[-1] = lax.optimization_barrier((new_up, new_down, kvs[-1]))
        kvs.append(halo_projections(new_up, new_down, weights))
        state_up, state_down = new_up, new_down
    o, dq, d3, d2, d1, d0 = attention(q, da, kvs[::-1], bias)

    kept, sent = outer_products(o, g, shot % 2)
    w_grad = reduce_outer(kept, sent)

    returned = back_projections(d3, weights, BF)
    terms = [back_projections(d2, weights, BF), back_projections(d1, weights, BF), last_projections(d0, dq, weights)]
    for term in terms:
        from_after = lax.ppermute(returned[0], "blk", down)
        from_before = lax.ppermute(returned[1], "blk", up)
        extra = jnp.where(at_last, returned[1], jnp.zeros_like(returned[1])).astype(F32)
        total = jnp.stack(
            [term[0].astype(F32) + from_after.astype(F32) + extra, term[1].astype(F32) + from_before.astype(F32)]
        )
        returned = total.astype(BF)
    return returned.reshape(tokens.shape), w_grad


def solution(mesh):
    placed = (
        P("dp", "blk", None, None, None),
        P("dp", None, None, None),
        P(),
        P("dp", "blk", None, None, None),
    )
    return jax.shard_map(
        per_device,
        mesh=mesh,
        in_specs=placed,
        out_specs=(P("dp", "blk", None, None, None), P("blk", "dp")),
        check_vma=False,
    )
```

```python
import jax
import jax.numpy as jnp
import numpy as np
from jax import lax
from jax.experimental import pallas as pl
from jax.experimental.pallas import tpu as pltpu
from jax.sharding import PartitionSpec as P

HEADS = 16
HEAD_DIM = 64
WIN = 4
BLOCK = 128
D = 1024
PAIR = 2 * HEAD_DIM
PAIRS_A_STEP = 4
TILE = 256
BF = jnp.bfloat16
F32 = jnp.float32

BARRED = -1e30
FREE = 3e38
SCALE = HEAD_DIM**-0.5
EXP2_SCALE = float(SCALE * np.log2(np.e))

NN = (((1,), (0,)), ((), ()))
NT = (((1,), (1,)), ((), ()))


def mm(a, b, dims=NN):
    return lax.dot_general(a, b, dims, preferred_element_type=F32)


def params(mib):
    return pltpu.CompilerParams(vmem_limit_bytes=mib * 2**20)


def cost(flops, moved, exps=0):
    return pl.CostEstimate(flops=flops, bytes_accessed=moved, transcendentals=exps)


def in_hbm(*arrays):
    return [pltpu.with_memory_space_constraint(a, pltpu.HBM) for a in arrays]


def in_vmem(*arrays):
    return [pltpu.with_memory_space_constraint(a, pltpu.VMEM) for a in arrays]


def weight_cols(which):
    return pl.BlockSpec((D, TILE), lambda t: (which, t))


def weight_rows(which):
    return pl.BlockSpec((TILE, D), lambda t: (which * (D // TILE) + t, 0))


def whole(shape):
    return pl.BlockSpec(shape, lambda t: (0,) * len(shape))


def own_kernel(x_ref, g_ref, wq_ref, wk_ref, wv_ref, wo_ref, q_ref, da_ref, kv_ref):
    x = x_ref[...].reshape(2 * BLOCK, D)
    g = g_ref[...].reshape(2 * BLOCK, D)
    q_ref[...] = mm(x, wq_ref[...]).astype(BF).reshape(2, BLOCK, TILE)
    da_ref[...] = mm(g, wo_ref[...], NT).astype(BF).reshape(2, BLOCK, TILE)
    kv_ref[0] = mm(x, wk_ref[...]).astype(BF).reshape(2, BLOCK, TILE)
    kv_ref[1] = mm(x, wv_ref[...]).astype(BF).reshape(2, BLOCK, TILE)


def own_projections(x, g, weights):
    rows = jax.ShapeDtypeStruct((2, BLOCK, D), BF)
    row_tile = pl.BlockSpec((2, BLOCK, TILE), lambda t: (0, 0, t))
    return pl.pallas_call(
        own_kernel,
        grid=(D // TILE,),
        in_specs=[
            whole((2, BLOCK, D)),
            whole((2, BLOCK, D)),
            weight_cols(0),
            weight_cols(1),
            weight_cols(2),
            weight_rows(3),
        ],
        out_specs=[row_tile, row_tile, pl.BlockSpec((2, 2, BLOCK, TILE), lambda t: (0, 0, 0, t))],
        out_shape=[rows, rows, jax.ShapeDtypeStruct((2, 2, BLOCK, D), BF)],
        compiler_params=params(12),
        cost_estimate=cost(8 * 2 * BLOCK * D * D, 8 * D * D + 12 * BLOCK * D),
        name="own_projections",
    )(*in_hbm(x, g, weights, weights, weights, weights))


def halo_kernel(up_ref, down_ref, wk_ref, wv_ref, kv_ref):
    x = jnp.concatenate([up_ref[...], down_ref[...]], axis=0)
    kv_ref[0] = mm(x, wk_ref[...]).astype(BF).reshape(2, BLOCK, TILE)
    kv_ref[1] = mm(x, wv_ref[...]).astype(BF).reshape(2, BLOCK, TILE)


def halo_projections(up, down, weights):
    return pl.pallas_call(
        halo_kernel,
        grid=(D // TILE,),
        in_specs=[whole((BLOCK, D)), whole((BLOCK, D)), weight_cols(1), weight_cols(2)],
        out_specs=pl.BlockSpec((2, 2, BLOCK, TILE), lambda t: (0, 0, 0, t)),
        out_shape=jax.ShapeDtypeStruct((2, 2, BLOCK, D), BF),
        compiler_params=params(10),
        cost_estimate=cost(4 * 2 * BLOCK * D * D, 4 * D * D + 12 * BLOCK * D),
        name="halo_projections",
    )(up, down, *in_vmem(weights, weights))


def attention_kernel(
    q_ref, da_ref, kv3_ref, kv2_ref, kv1_ref, kv0_ref, bias_ref,
    out_ref, dq_ref, d3_ref, d2_ref, d1_ref, d0_ref,
):
    first = lax.broadcasted_iota(jnp.int32, (BLOCK, PAIR), 1) < HEAD_DIM
    kv_refs = (kv3_ref, kv2_ref, kv1_ref, kv0_ref)
    d_refs = (d3_ref, d2_ref, d1_ref, d0_ref)
    lanes = [slice(i * PAIR, (i + 1) * PAIR) for i in range(PAIRS_A_STEP)]

    def split(rows):
        zero = jnp.zeros_like(rows)
        return jnp.concatenate([jnp.where(first, rows, zero), jnp.where(first, zero, rows)], axis=0)

    def merge(rows):
        return jnp.where(first, rows[:BLOCK], rows[BLOCK:])

    def twice(rows):
        return jnp.concatenate([rows, rows], axis=0)

    bias = twice(bias_ref[0])
    ones = jnp.ones((WIN * BLOCK, PAIR), BF)
    keys = [jnp.concatenate([ref[0, 0, :, c] for ref in kv_refs], axis=0) for c in lanes]
    values = [jnp.concatenate([ref[1, 0, :, c] for ref in kv_refs], axis=0) for c in lanes]
    queries = [split(q_ref[0, :, c]) for c in lanes]
    d_attn = [split(da_ref[0, :, c]) for c in lanes]
    scores = [jnp.minimum(mm(q, k, NT), bias) for q, k in zip(queries, keys)]
    tops = [jnp.max(s, axis=1, keepdims=True) for s in scores]
    terms = [jnp.exp2((s - t) * EXP2_SCALE).astype(BF) for s, t in zip(scores, tops)]
    sums = [mm(t, jnp.concatenate([v, ones], axis=1)) for t, v in zip(terms, values)]
    shares = [1.0 / s[:, PAIR:] for s in sums]
    outs = [merge(s[:, :PAIR] * r).astype(BF) for s, r in zip(sums, shares)]
    for c, o in zip(lanes, outs):
        out_ref[0, :, c] = o
    scaled = [d.astype(F32) * r for d, r in zip(d_attn, shares)]
    deltas = [
        jnp.sum(d * twice(o.astype(F32)), axis=1, keepdims=True) for d, o in zip(scaled, outs)
    ]
    scaled = [d.astype(BF) for d in scaled]
    d_probs = [mm(d, v, NT) for d, v in zip(scaled, values)]
    d_scores = [(p - d).astype(BF) * t for p, d, t in zip(d_probs, deltas, terms)]
    d_values = [mm(d.T, t).astype(BF).T for d, t in zip(scaled, terms)]
    d_queries = [merge(mm(d, k)) for d, k in zip(d_scores, keys)]
    for c, d in zip(lanes, d_queries):
        dq_ref[0, :, c] = (d * SCALE).astype(BF)
    d_keys = [(mm(q.T, d) * SCALE).astype(BF).T for q, d in zip(queries, d_scores)]
    for c, dk, dv in zip(lanes, d_keys, d_values):
        for i, ref in enumerate(d_refs):
            ref[0, 0, :, c] = dk[i * BLOCK : (i + 1) * BLOCK]
            ref[1, 0, :, c] = dv[i * BLOCK : (i + 1) * BLOCK]


def attention(q, da, kvs, bias):
    rows = jax.ShapeDtypeStruct((2, BLOCK, D), BF)
    pairs = jax.ShapeDtypeStruct((2, 2, BLOCK, D), BF)
    width = PAIRS_A_STEP * PAIR
    row_spec = pl.BlockSpec((1, BLOCK, width), lambda h, p: (h, 0, p))
    pair_spec = pl.BlockSpec((2, 1, BLOCK, width), lambda h, p: (0, h, 0, p))
    bias_spec = pl.BlockSpec((1, BLOCK, WIN * BLOCK), lambda h, p: (h, 0, 0))
    return pl.pallas_call(
        attention_kernel,
        grid=(2, D // width),
        in_specs=[row_spec, row_spec] + [pair_spec] * 4 + [bias_spec],
        out_specs=[row_spec, row_spec] + [pair_spec] * 4,
        out_shape=[rows, rows] + [pairs] * 4,
        compiler_params=params(24),
        cost_estimate=cost(2 * 10 * BLOCK * WIN * BLOCK * D * 2, 12 * 2**20, 2**21),
        name="attention",
    )(*in_vmem(q, da, *kvs, bias))


def back_kernel(d_ref, wk_ref, wv_ref, out_ref):
    rows = mm(d_ref[0].reshape(2 * BLOCK, D), wk_ref[...], NT)
    rows += mm(d_ref[1].reshape(2 * BLOCK, D), wv_ref[...], NT)
    out_ref[...] = rows.reshape(2, BLOCK, TILE).astype(out_ref.dtype)


def back_projections(d, weights, dtype):
    return pl.pallas_call(
        back_kernel,
        grid=(D // TILE,),
        in_specs=[whole((2, 2, BLOCK, D)), weight_rows(1), weight_rows(2)],
        out_specs=pl.BlockSpec((2, BLOCK, TILE), lambda t: (0, 0, t)),
        out_shape=jax.ShapeDtypeStruct((2, BLOCK, D), dtype),
        compiler_params=params(10),
        cost_estimate=cost(4 * 2 * BLOCK * D * D, 4 * D * D + 12 * BLOCK * D),
        name="back_projections",
    )(*in_vmem(d, weights, weights))


def last_kernel(d_ref, dq_ref, wq_ref, wk_ref, wv_ref, out_ref):
    rows = mm(dq_ref[...].reshape(2 * BLOCK, D), wq_ref[...], NT)
    rows += mm(d_ref[0].reshape(2 * BLOCK, D), wk_ref[...], NT)
    rows += mm(d_ref[1].reshape(2 * BLOCK, D), wv_ref[...], NT)
    out_ref[...] = rows.reshape(2, BLOCK, TILE)


def last_projections(d, dq, weights):
    return pl.pallas_call(
        last_kernel,
        grid=(D // TILE,),
        in_specs=[
            whole((2, 2, BLOCK, D)),
            whole((2, BLOCK, D)),
            weight_rows(0),
            weight_rows(1),
            weight_rows(2),
        ],
        out_specs=pl.BlockSpec((2, BLOCK, TILE), lambda t: (0, 0, t)),
        out_shape=jax.ShapeDtypeStruct((2, BLOCK, D), F32),
        compiler_params=params(12),
        cost_estimate=cost(6 * 2 * BLOCK * D * D, 6 * D * D + 16 * BLOCK * D),
        name="last_projections",
    )(*in_vmem(d, dq, weights, weights, weights))


def outer_kernel(core_ref, o_ref, keep_ref, send_ref, kept_ref, sent_ref):
    o_t = o_ref[...].reshape(2 * BLOCK, D).T
    for g_ref, r_ref in ((send_ref, sent_ref), (keep_ref, kept_ref)):
        r_ref[0] = mm(o_t, g_ref[...].reshape(2 * BLOCK, TILE)).astype(BF)


def outer_products(o, g, core):
    result = jax.ShapeDtypeStruct((2, D, TILE), BF)
    result_spec = pl.BlockSpec((1, D, TILE), lambda y, c: (y, 0, 0))
    return pl.pallas_call(
        outer_kernel,
        grid_spec=pltpu.PrefetchScalarGridSpec(
            num_scalar_prefetch=1,
            grid=(2,),
            in_specs=[
                pl.BlockSpec((2, BLOCK, D), lambda y, c: (0, 0, 0)),
                pl.BlockSpec((2, BLOCK, TILE), lambda y, c: (0, 0, 2 * y + c[0])),
                pl.BlockSpec((2, BLOCK, TILE), lambda y, c: (0, 0, 2 * y + 1 - c[0])),
            ],
            out_specs=[result_spec, result_spec],
        ),
        out_shape=[result, result],
        compiler_params=params(12),
        cost_estimate=cost(4 * BLOCK * D * D, 2 * D * D + 8 * BLOCK * D),
        name="outer_products",
    )(core, *in_vmem(o, g, g))


def place(y, x, z, core):
    return ((y % 2) * 32 + x * 8 + z) * 4 + (y // 2) * 2 + core


CORE_PAIRS = [(i, i ^ 1) for i in range(4)]
PLANES = [
    [place(y, x, z, core) for y in range(4) for x in range(4)] for z in range(8) for core in range(2)
]
LINES = [[32 * y + 8 * x + z for z in range(8)] for y in range(2) for x in range(4)]


def add(a, b):
    return (a.astype(F32) + b.astype(F32)).astype(BF)


def sum_over_plane(total):
    total = total.reshape(16, 8 * 16, TILE)
    total = lax.all_to_all(total, ("blk", "dp"), 0, 0, axis_index_groups=PLANES)
    return jnp.sum(total.astype(F32), axis=0).astype(BF).reshape(8, 16, TILE)


def sum_over_line(total):
    total = lax.all_to_all(total, "blk", 0, 0, axis_index_groups=LINES)
    return jnp.sum(total.astype(F32), axis=0)


def window_validity(key_valid, both):
    seq_valid = jnp.concatenate([key_valid[0, :, 0], jnp.flip(key_valid[0, :, 1], axis=0)], axis=0)
    seq_valid = jnp.concatenate([jnp.zeros((WIN - 1, BLOCK), jnp.int32), seq_valid], axis=0)
    return jnp.stack(
        [lax.dynamic_slice_in_dim(seq_valid, both[i], WIN, 0).reshape(WIN * BLOCK) for i in range(2)]
    )


def score_limits(valid, both):
    q_pos = jnp.arange(BLOCK, dtype=jnp.int32)[None, :, None]
    k_pos = (jnp.arange(WIN * BLOCK, dtype=jnp.int32) - (WIN - 1) * BLOCK)[None, None, :]
    inside = k_pos + both[:, None, None] * BLOCK >= 0
    allowed = inside & (k_pos <= q_pos) & ((valid[:, None, :] == 1) | (k_pos == q_pos))
    return jnp.where(allowed, FREE, BARRED).astype(F32)


def per_device(tokens, key_valid, weights, out_grad):
    position = lax.axis_index("blk")
    shot = lax.axis_index("dp")
    at_first = position == 0
    at_last = position == 63
    up = [(i, (i + 1) % 64) for i in range(64)]
    down = [(t, s) for s, t in up]
    x = tokens.reshape(2, BLOCK, D)
    g = out_grad.reshape(2, BLOCK, D)

    both = jnp.stack([position, 2 * 64 - 1 - position])
    valid = window_validity(key_valid, both)
    core = (shot % 2).reshape(1)
    x, g, valid, both, core, at_first, at_last = lax.optimization_barrier(
        (x, g, valid, both, core, at_first, at_last)
    )
    bias = score_limits(valid, both)
    q, da, kv0 = own_projections(x, g, weights)
    kvs = [kv0]
    state_up, state_down = x[0], x[1]
    for _ in range(WIN - 1):
        new_up = lax.ppermute(state_up, "blk", up)
        new_down = jnp.where(at_last, state_up, lax.ppermute(state_down, "blk", down))
        new_up, new_down, kvs[-1] = lax.optimization_barrier((new_up, new_down, kvs[-1]))
        kvs.append(halo_projections(new_up, new_down, weights))
        state_up, state_down = new_up, new_down
    o, dq, d3, d2, d1, d0 = attention(q, da, kvs[::-1], bias)

    returned = back_projections(d3, weights, BF)
    o, returned = lax.optimization_barrier((o, returned))
    kept, sent = outer_products(o, g, core)
    chip_sum = add(kept, lax.ppermute(sent, "dp", CORE_PAIRS))
    d2, chip_sum = lax.optimization_barrier((d2, chip_sum))
    terms = [back_projections(d2, weights, BF), back_projections(d1, weights, BF), last_projections(d0, dq, weights)]
    for hop, term in enumerate(terms):
        from_after = lax.ppermute(returned[0], "blk", down)
        from_before = lax.ppermute(returned[1], "blk", up)
        extra = jnp.where(at_last, returned[1], jnp.zeros_like(returned[1])).astype(F32)
        from_before = jnp.where(at_first, jnp.zeros_like(from_before), from_before)
        total = jnp.stack(
            [term[0].astype(F32) + from_after.astype(F32) + extra, term[1].astype(F32) + from_before.astype(F32)]
        )
        returned = total.astype(BF)
        if hop == 0:
            returned, chip_sum = lax.optimization_barrier((returned, chip_sum))
            plane_sum = sum_over_plane(chip_sum)
            returned, plane_sum, terms[1], terms[2] = lax.optimization_barrier(
                (returned, plane_sum, terms[1], terms[2])
            )
            w_grad = sum_over_line(plane_sum)
        if hop == 1:
            returned, w_grad = lax.optimization_barrier((returned, w_grad))
    return returned.reshape(tokens.shape), w_grad


def solution(mesh):
    placed = (
        P("dp", "blk", None, None, None),
        P("dp", None, None, None),
        P(),
        P("dp", "blk", None, None, None),
    )
    return jax.shard_map(
        per_device,
        mesh=mesh,
        in_specs=placed,
        out_specs=(P("dp", "blk", None, None, None), P("blk", "dp")),
        check_vma=False,
    )
```

```python
import jax
import jax.numpy as jnp
import numpy as np
from jax import lax
from jax.experimental import pallas as pl
from jax.experimental.pallas import tpu as pltpu
from jax.sharding import PartitionSpec as P

HEADS = 16
HEAD_DIM = 64
WIN = 4
BLOCK = 128
D = 1024
PAIR = 2 * HEAD_DIM
PAIRS_A_STEP = 4
TILE = 256
BF = jnp.bfloat16
F32 = jnp.float32

BARRED = -1e30
FREE = 3e38
SCALE = HEAD_DIM**-0.5
EXP2_SCALE = float(SCALE * np.log2(np.e))

NN = (((1,), (0,)), ((), ()))
NT = (((1,), (1,)), ((), ()))


def mm(a, b, dims=NN):
    return lax.dot_general(a, b, dims, preferred_element_type=F32)


def params(mib):
    return pltpu.CompilerParams(vmem_limit_bytes=mib * 2**20)


def cost(flops, moved, exps=0):
    return pl.CostEstimate(flops=flops, bytes_accessed=moved, transcendentals=exps)


def in_hbm(*arrays):
    return [pltpu.with_memory_space_constraint(a, pltpu.HBM) for a in arrays]


def in_vmem(*arrays):
    return [pltpu.with_memory_space_constraint(a, pltpu.VMEM) for a in arrays]


def weight_cols(which):
    return pl.BlockSpec((D, TILE), lambda t: (which, t))


def weight_rows(which):
    return pl.BlockSpec((TILE, D), lambda t: (which * (D // TILE) + t, 0))


def whole(shape):
    return pl.BlockSpec(shape, lambda t: (0,) * len(shape))


def own_kernel(x_ref, wk_ref, wv_ref, kv_ref, wk_out, wv_out):
    wk_out[...] = wk_ref[...]
    wv_out[...] = wv_ref[...]
    x = x_ref[...].reshape(2 * BLOCK, D)
    kv_ref[0] = mm(x, wk_ref[...]).astype(BF).reshape(2, BLOCK, TILE)
    kv_ref[1] = mm(x, wv_ref[...]).astype(BF).reshape(2, BLOCK, TILE)


def own_projections(x, weights):
    return pl.pallas_call(
        own_kernel,
        grid=(D // TILE,),
        in_specs=[whole((2, BLOCK, D)), weight_cols(1), weight_cols(2)],
        out_specs=[pl.BlockSpec((2, 2, BLOCK, TILE), lambda t: (0, 0, 0, t))] + [weight_cols(0)] * 2,
        out_shape=[jax.ShapeDtypeStruct((2, 2, BLOCK, D), BF)] + [jax.ShapeDtypeStruct((D, D), BF)] * 2,
        compiler_params=params(12),
        cost_estimate=cost(8 * 2 * BLOCK * D * D, 12 * D * D + 12 * BLOCK * D),
        name="own_projections",
    )(*in_hbm(x, weights, weights))


def query_kernel(x_ref, g_ref, wq_ref, wo_ref, q_ref, da_ref, wq_out):
    wq_out[...] = wq_ref[...]
    x = x_ref[...].reshape(2 * BLOCK, D)
    g = g_ref[...].reshape(2 * BLOCK, D)
    q_ref[...] = mm(x, wq_ref[...]).astype(BF).reshape(2, BLOCK, TILE)
    da_ref[...] = mm(g, wo_ref[...], NT).astype(BF).reshape(2, BLOCK, TILE)


def query_projections(x, g, weights):
    rows = jax.ShapeDtypeStruct((2, BLOCK, D), BF)
    row_tile = pl.BlockSpec((2, BLOCK, TILE), lambda t: (0, 0, t))
    return pl.pallas_call(
        query_kernel,
        grid=(D // TILE,),
        in_specs=[whole((2, BLOCK, D)), whole((2, BLOCK, D)), weight_cols(0), weight_rows(3)],
        out_specs=[row_tile, row_tile, weight_cols(0)],
        out_shape=[rows, rows, jax.ShapeDtypeStruct((D, D), BF)],
        compiler_params=params(12),
        cost_estimate=cost(8 * 2 * BLOCK * D * D, 12 * D * D + 12 * BLOCK * D),
        name="query_projections",
    )(*in_hbm(x, g, weights, weights))


def halo_kernel(up_ref, down_ref, wk_ref, wv_ref, kv_ref):
    x = jnp.concatenate([up_ref[...], down_ref[...]], axis=0)
    kv_ref[0] = mm(x, wk_ref[...]).astype(BF).reshape(2, BLOCK, TILE)
    kv_ref[1] = mm(x, wv_ref[...]).astype(BF).reshape(2, BLOCK, TILE)


def halo_projections(up, down, wk, wv):
    return pl.pallas_call(
        halo_kernel,
        grid=(D // TILE,),
        in_specs=[whole((BLOCK, D)), whole((BLOCK, D)), weight_cols(0), weight_cols(0)],
        out_specs=pl.BlockSpec((2, 2, BLOCK, TILE), lambda t: (0, 0, 0, t)),
        out_shape=jax.ShapeDtypeStruct((2, 2, BLOCK, D), BF),
        compiler_params=params(10),
        cost_estimate=cost(4 * 2 * BLOCK * D * D, 4 * D * D + 12 * BLOCK * D),
        name="halo_projections",
    )(up, down, *in_vmem(wk, wv))


def attention_kernel(
    place, valid_ref, q_ref, da_ref, kv3_ref, kv2_ref, kv1_ref, kv0_ref,
    out_ref, dq_ref, d3_ref, d2_ref, d1_ref, d0_ref,
):
    first = lax.broadcasted_iota(jnp.int32, (BLOCK, PAIR), 1) < HEAD_DIM
    kv_refs = (kv3_ref, kv2_ref, kv1_ref, kv0_ref)
    d_refs = (d3_ref, d2_ref, d1_ref, d0_ref)
    lanes = [slice(i * PAIR, (i + 1) * PAIR) for i in range(PAIRS_A_STEP)]

    def split(rows):
        zero = jnp.zeros_like(rows)
        return jnp.concatenate([jnp.where(first, rows, zero), jnp.where(first, zero, rows)], axis=0)

    def merge(rows):
        return jnp.where(first, rows[:BLOCK], rows[BLOCK:])

    def twice(rows):
        return jnp.concatenate([rows, rows], axis=0)

    block = jnp.where(pl.program_id(0) == 0, place[0], 127 - place[0])
    limits = []
    for back in range(WIN - 1, -1, -1):
        key_block = block - back
        slot = jnp.maximum(jnp.where(key_block < 64, key_block, 127 - key_block), 0)
        halves = valid_ref[pl.ds(slot, 1)].reshape(2, BLOCK)
        serves = jnp.where(key_block < 64, halves[:1], halves[1:])
        limit = jnp.where((serves == 1) & (key_block >= 0), FREE, BARRED)
        limits.append(jnp.broadcast_to(limit, (BLOCK, BLOCK)))
    row = lax.broadcasted_iota(jnp.int32, (BLOCK, BLOCK), 0)
    column = lax.broadcasted_iota(jnp.int32, (BLOCK, BLOCK), 1)
    limits[-1] = jnp.where(row == column, FREE, jnp.where(row > column, limits[-1], BARRED))
    bias = twice(jnp.concatenate(limits, axis=1))
    ones = jnp.ones((WIN * BLOCK, PAIR), BF)
    keys = [jnp.concatenate([ref[0, 0, :, c] for ref in kv_refs], axis=0) for c in lanes]
    values = [jnp.concatenate([ref[1, 0, :, c] for ref in kv_refs], axis=0) for c in lanes]
    queries = [split(q_ref[0, :, c]) for c in lanes]
    d_attn = [split(da_ref[0, :, c]) for c in lanes]
    scores = [jnp.minimum(mm(q, k, NT), bias) for q, k in zip(queries, keys)]
    tops = [jnp.max(s, axis=1, keepdims=True) for s in scores]
    terms = [jnp.exp2((s - t) * EXP2_SCALE).astype(BF) for s, t in zip(scores, tops)]
    sums = [mm(t, jnp.concatenate([v, ones], axis=1)) for t, v in zip(terms, values)]
    shares = [1.0 / s[:, PAIR:] for s in sums]
    outs = [merge(s[:, :PAIR] * r).astype(BF) for s, r in zip(sums, shares)]
    for c, o in zip(lanes, outs):
        out_ref[0, :, c] = o
    scaled = [d.astype(F32) * r for d, r in zip(d_attn, shares)]
    deltas = [
        jnp.sum(d * twice(o.astype(F32)), axis=1, keepdims=True) for d, o in zip(scaled, outs)
    ]
    scaled = [d.astype(BF) for d in scaled]
    d_probs = [mm(d, v, NT) for d, v in zip(scaled, values)]
    d_scores = [(p - d).astype(BF) * t for p, d, t in zip(d_probs, deltas, terms)]
    d_values = [mm(d.T, t).astype(BF).T for d, t in zip(scaled, terms)]
    d_queries = [merge(mm(d, k)) for d, k in zip(d_scores, keys)]
    for c, d in zip(lanes, d_queries):
        dq_ref[0, :, c] = (d * SCALE).astype(BF)
    d_keys = [(mm(q.T, d) * SCALE).astype(BF).T for q, d in zip(queries, d_scores)]
    for c, dk, dv in zip(lanes, d_keys, d_values):
        for i, ref in enumerate(d_refs):
            ref[0, 0, :, c] = dk[i * BLOCK : (i + 1) * BLOCK]
            ref[1, 0, :, c] = dv[i * BLOCK : (i + 1) * BLOCK]


def attention(place, key_valid, q, da, kvs):
    rows = jax.ShapeDtypeStruct((2, BLOCK, D), BF)
    pairs = jax.ShapeDtypeStruct((2, 2, BLOCK, D), BF)
    width = PAIRS_A_STEP * PAIR
    row_spec = pl.BlockSpec((1, BLOCK, width), lambda h, p, s: (h, 0, p))
    pair_spec = pl.BlockSpec((2, 1, BLOCK, width), lambda h, p, s: (0, h, 0, p))
    valid_spec = pl.BlockSpec((64, 2, BLOCK), lambda h, p, s: (0, 0, 0))
    return pl.pallas_call(
        attention_kernel,
        grid_spec=pltpu.PrefetchScalarGridSpec(
            num_scalar_prefetch=1,
            grid=(2, D // width),
            in_specs=[valid_spec, row_spec, row_spec] + [pair_spec] * 4,
            out_specs=[row_spec, row_spec] + [pair_spec] * 4,
        ),
        out_shape=[rows, rows] + [pairs] * 4,
        compiler_params=params(24),
        cost_estimate=cost(2 * 10 * BLOCK * WIN * BLOCK * D * 2, 12 * 2**20, 2**21),
        name="attention",
    )(place, key_valid, *in_vmem(q, da, *kvs))


def back_kernel(d_ref, wk_ref, wv_ref, first_ref, second_ref):
    rows = mm(d_ref[0].reshape(2 * BLOCK, D), wk_ref[...], NT)
    rows += mm(d_ref[1].reshape(2 * BLOCK, D), wv_ref[...], NT)
    first_ref[...] = rows[:BLOCK].astype(BF)
    second_ref[...] = rows[BLOCK:].astype(BF)


def back_projections(d, wk, wv):
    return pl.pallas_call(
        back_kernel,
        grid=(D // TILE,),
        in_specs=[whole((2, 2, BLOCK, D)), weight_rows(0), weight_rows(0)],
        out_specs=[pl.BlockSpec((BLOCK, TILE), lambda t: (0, t))] * 2,
        out_shape=[jax.ShapeDtypeStruct((BLOCK, D), BF)] * 2,
        compiler_params=params(10),
        cost_estimate=cost(4 * 2 * BLOCK * D * D, 4 * D * D + 12 * BLOCK * D),
        name="back_projections",
    )(*in_vmem(d, wk, wv))


def last_kernel(d_ref, dq_ref, wq_ref, wk_ref, wv_ref, first_ref, second_ref):
    rows = mm(dq_ref[...].reshape(2 * BLOCK, D), wq_ref[...], NT)
    rows += mm(d_ref[0].reshape(2 * BLOCK, D), wk_ref[...], NT)
    rows += mm(d_ref[1].reshape(2 * BLOCK, D), wv_ref[...], NT)
    first_ref[...] = rows[:BLOCK]
    second_ref[...] = rows[BLOCK:]


def last_projections(d, dq, wq, wk, wv):
    return pl.pallas_call(
        last_kernel,
        grid=(D // TILE,),
        in_specs=[
            whole((2, 2, BLOCK, D)),
            whole((2, BLOCK, D)),
            weight_rows(0),
            weight_rows(0),
            weight_rows(0),
        ],
        out_specs=[pl.BlockSpec((BLOCK, TILE), lambda t: (0, t))] * 2,
        out_shape=[jax.ShapeDtypeStruct((BLOCK, D), F32)] * 2,
        compiler_params=params(12),
        cost_estimate=cost(6 * 2 * BLOCK * D * D, 6 * D * D + 16 * BLOCK * D),
        name="last_projections",
    )(*in_vmem(d, dq, wq, wk, wv))


def outer_kernel(core_ref, o_ref, keep_ref, send_ref, kept_ref, sent_ref):
    o_t = o_ref[...].reshape(2 * BLOCK, D).T
    for g_ref, r_ref in ((send_ref, sent_ref), (keep_ref, kept_ref)):
        r_ref[0] = mm(o_t, g_ref[...].reshape(2 * BLOCK, TILE)).astype(BF)


def outer_products(o, g, core):
    result = jax.ShapeDtypeStruct((2, D, TILE), BF)
    result_spec = pl.BlockSpec((1, D, TILE), lambda y, c: (y, 0, 0))
    return pl.pallas_call(
        outer_kernel,
        grid_spec=pltpu.PrefetchScalarGridSpec(
            num_scalar_prefetch=1,
            grid=(2,),
            in_specs=[
                pl.BlockSpec((2, BLOCK, D), lambda y, c: (0, 0, 0)),
                pl.BlockSpec((2, BLOCK, TILE), lambda y, c: (0, 0, 2 * y + c[0])),
                pl.BlockSpec((2, BLOCK, TILE), lambda y, c: (0, 0, 2 * y + 1 - c[0])),
            ],
            out_specs=[result_spec, result_spec],
        ),
        out_shape=[result, result],
        compiler_params=params(12),
        cost_estimate=cost(4 * BLOCK * D * D, 2 * D * D + 8 * BLOCK * D),
        name="outer_products",
    )(core, *in_vmem(o, g, g))


def hop_kernel(place_ref, t0_ref, t1_ref, after_ref, before_ref, state_ref, out_ref):
    blk = place_ref[0]
    folded = jnp.where(blk == 63, state_ref[...].astype(F32), 0.0)
    before = jnp.where(blk == 0, 0.0, before_ref[...].astype(F32))
    first = t0_ref[...].astype(F32) + after_ref[...].astype(F32) + folded
    out_ref[0] = first.astype(BF)
    out_ref[1] = (t1_ref[...].astype(F32) + before).astype(BF)


def inner_hop_kernel(place_ref, t0_ref, t1_ref, after_ref, before_ref, state_ref, first_ref, second_ref):
    blk = place_ref[0]
    folded = jnp.where(blk == 63, state_ref[...].astype(F32), 0.0)
    before = jnp.where(blk == 0, 0.0, before_ref[...].astype(F32))
    first = t0_ref[...].astype(F32) + after_ref[...].astype(F32) + folded
    first_ref[...] = first.astype(BF)
    second_ref[...] = (t1_ref[...].astype(F32) + before).astype(BF)


def hop_back(place, terms, after, before, state, last):
    spec = pl.BlockSpec((BLOCK, D // 2), lambda t, p: (0, t))
    if last:
        out_specs = pl.BlockSpec((2, BLOCK, D // 2), lambda t, p: (0, 0, t))
        out_shape = jax.ShapeDtypeStruct((2, BLOCK, D), BF)
    else:
        out_specs = [spec] * 2
        out_shape = [jax.ShapeDtypeStruct((BLOCK, D), BF)] * 2
    return pl.pallas_call(
        hop_kernel if last else inner_hop_kernel,
        grid_spec=pltpu.PrefetchScalarGridSpec(
            num_scalar_prefetch=1, grid=(2,), in_specs=[spec] * 5, out_specs=out_specs
        ),
        out_shape=out_shape,
        compiler_params=params(6),
        cost_estimate=cost(8 * BLOCK * D, 14 * BLOCK * D),
        name="hop_back",
    )(place, *in_vmem(*terms, after, before, state))


def chip(y, x, z, core):
    return ((y % 2) * 32 + x * 8 + z) * 4 + (y // 2) * 2 + core


CORE_PAIRS = [(i, i ^ 1) for i in range(4)]
LINES = [[32 * y + 8 * x + z for z in range(8)] for y in range(2) for x in range(4)]
FLIP = ((1, 0, 3, 2), (3, 2, 1, 0))


def halving_pairs(second, turn):
    pairs = []
    for y in range(4):
        for x in range(4):
            for z in range(8):
                for core in range(2):
                    along_x = (core == 0) != second
                    to = (y, FLIP[turn][x]) if along_x else (FLIP[turn][y], x)
                    pairs.append((chip(y, x, z, core), chip(*to, z, core)))
    return pairs


SHARE = 128


def places(position, shot):
    def ring(i):
        outer = (i == 0) | (i == 3)
        keep = [jnp.where(outer, 0, 1), jnp.where(outer, 3, 2)]
        send = [jnp.where(outer, 1, 0), jnp.where(outer, 2, 3)]
        return keep + send + [i // 2, 1 - i // 2]

    core = shot % 2
    x = (position // 8) % 4
    y = (shot // 2) * 2 + position // 32
    first, second = jnp.where(core == 0, x, y), jnp.where(core == 0, y, x)
    return jnp.stack([position, core] + ring(first) + ring(second)).astype(jnp.int32)


FIRST, SECOND = 2, 8


def total(a, b):
    return (a.astype(F32) + b.astype(F32)).astype(BF)


def split_core(place, kept_ref, other_ref, keep_ref, send_ref):
    for out_ref, at in ((keep_ref, FIRST), (send_ref, FIRST + 2)):
        for i in range(2):
            for j in range(4):
                first = place[at + i]
                y = pl.ds(jnp.where(place[1] == 0, j, first), 1)
                x = pl.ds(jnp.where(place[1] == 0, first, j), 1)
                out_ref[i : i + 1, j : j + 1] = total(kept_ref[y, x], other_ref[y, x])


def split_first(place, kept_ref, moved_ref, keep_ref, send_ref):
    for j, out_ref in enumerate((keep_ref, send_ref)):
        i = pl.ds(place[FIRST + 4 + j], 1)
        out_ref[...] = total(kept_ref[i], moved_ref[i])


def split_second(place, kept_ref, moved_ref, keep_ref, send_ref):
    for out_ref, at in ((keep_ref, SECOND), (send_ref, SECOND + 2)):
        for j in range(2):
            i = pl.ds(place[at + j], 1)
            out_ref[:, j : j + 1] = total(kept_ref[:, i], moved_ref[:, i])


def split_third(place, kept_ref, moved_ref, keep_ref, send_ref):
    for j, out_ref in enumerate((keep_ref, send_ref)):
        i = pl.ds(place[SECOND + 4 + j], 1)
        out_ref[...] = total(kept_ref[:, i], moved_ref[:, i])


def join_last(place, kept_ref, moved_ref, out_ref):
    out_ref[...] = total(kept_ref[...], moved_ref[...])


def halving(kernel, place, arrays, shapes):
    vmem = pl.BlockSpec(memory_space=pltpu.VMEM)
    return pl.pallas_call(
        kernel,
        in_specs=[pl.BlockSpec(memory_space=pltpu.SMEM)] + [vmem] * len(arrays),
        out_specs=[vmem] * len(shapes),
        out_shape=[jax.ShapeDtypeStruct(shape + (SHARE, TILE), BF) for shape in shapes],
        compiler_params=params(8),
        cost_estimate=cost(2**20, 2**20),
        name=kernel.__name__,
    )(place, *arrays)


def halve_core(place, kept, other):
    arrays = [v.reshape(4, 4, SHARE, TILE) for v in (kept, other)]
    return halving(split_core, place, arrays, [(2, 4)] * 2)


HALVINGS = (
    (split_first, halving_pairs(False, 0), [(1, 4)] * 2),
    (split_second, halving_pairs(False, 1), [(1, 2)] * 2),
    (split_third, halving_pairs(True, 0), [(1, 1)] * 2),
    (join_last, halving_pairs(True, 1), [(1, 1)]),
)


def halve(turn, place, pieces):
    kernel, pairs, shapes = HALVINGS[turn]
    keep, send = pieces
    return halving(kernel, place, [keep, lax.ppermute(send, ("blk", "dp"), pairs)], shapes)


def sum_over_line(total):
    total = lax.all_to_all(total.reshape(8, 16, TILE), "blk", 0, 0, axis_index_groups=LINES)
    return jnp.sum(total.astype(F32), axis=0)


def per_device(tokens, key_valid, weights, out_grad):
    position = lax.axis_index("blk")
    shot = lax.axis_index("dp")
    up = [(i, (i + 1) % 64) for i in range(64)]
    down = [(t, s) for s, t in up]
    x = tokens.reshape(2, BLOCK, D)
    g = out_grad.reshape(2, BLOCK, D)

    core = (shot % 2).reshape(1)
    place = places(position, shot)
    at_last = position == 63
    own, core, place, at_last = lax.optimization_barrier((x, core, place, at_last))
    kv0, wk, wv = own_projections(own, weights)
    kvs = [kv0]
    state_up, state_down = x[0], x[1]
    for hop_index in range(WIN - 1):
        new_up = lax.ppermute(state_up, "blk", up)
        new_down = lax.ppermute(state_down, "blk", down)
        if hop_index == 1:
            q, da, wq, kvs[-1] = lax.optimization_barrier((*query_projections(own, g, weights), kvs[-1]))
            new_up, new_down, q = lax.optimization_barrier((new_up, new_down, q))
        new_up, new_down, kvs[-1] = lax.optimization_barrier((new_up, new_down, kvs[-1]))
        new_down = jnp.where(at_last, state_up, new_down)
        kvs.append(halo_projections(new_up, new_down, wk, wv))
        state_up, state_down = new_up, new_down
    o, dq, d3, d2, d1, d0 = attention(place, key_valid.reshape(64, 2, BLOCK), q, da, kvs[::-1])

    def hop(state):
        return lax.ppermute(state[0], "blk", down), lax.ppermute(state[1], "blk", up)

    kept, sent = outer_products(o, g, core)
    other = lax.ppermute(sent, "dp", CORE_PAIRS)
    d2, _ = lax.optimization_barrier((d2, sent))
    terms = back_projections(d2, wk, wv)
    kept, other, terms = lax.optimization_barrier((kept, other, terms))
    pieces = halve_core(place, kept, other)
    d3, pieces = lax.optimization_barrier((d3, pieces))
    state = back_projections(d3, wk, wv)

    moved = hop(state)
    d1, state = lax.optimization_barrier((d1, state))
    later = back_projections(d1, wk, wv)
    pieces = halve(0, place, pieces)
    moved, pieces, later = lax.optimization_barrier((moved, pieces, later))
    state = hop_back(place, terms, *moved, state[1], False)

    moved = hop(state)
    d0, state = lax.optimization_barrier((d0, state))
    last = last_projections(d0, dq, wq, wk, wv)
    pieces = halve(2, place, halve(1, place, pieces))
    moved, pieces, last = lax.optimization_barrier((moved, pieces, last))
    state = hop_back(place, later, *moved, state[1], False)

    moved = hop(state)
    (plane_sum,) = halve(3, place, pieces)
    moved, plane_sum = lax.optimization_barrier((moved, plane_sum))
    grad_tokens = hop_back(place, last, *moved, state[1], True)
    w_grad = sum_over_line(plane_sum)
    return grad_tokens.reshape(tokens.shape), w_grad


def solution(mesh):
    placed = (
        P("dp", "blk", None, None, None),
        P("dp", None, None, None),
        P(),
        P("dp", "blk", None, None, None),
    )
    return jax.shard_map(
        per_device,
        mesh=mesh,
        in_specs=placed,
        out_specs=(P("dp", "blk", None, None, None), P("blk", "dp")),
        check_vma=False,
    )
```

```python
import jax
import jax.numpy as jnp
import numpy as np
from jax import lax
from jax.experimental import pallas as pl
from jax.experimental.pallas import tpu as pltpu
from jax.sharding import PartitionSpec as P

HEADS = 16
HEAD_DIM = 64
WIN = 4
BLOCK = 128
D = 1024
PAIR = 2 * HEAD_DIM
PAIRS_A_STEP = 4
TILE = 256
BF = jnp.bfloat16
F32 = jnp.float32

BARRED = -1e30
FREE = 3e38
SCALE = HEAD_DIM**-0.5
EXP2_SCALE = float(SCALE * np.log2(np.e))

NN = (((1,), (0,)), ((), ()))
NT = (((1,), (1,)), ((), ()))


def mm(a, b, dims=NN):
    return lax.dot_general(a, b, dims, preferred_element_type=F32)


def params(mib):
    return pltpu.CompilerParams(vmem_limit_bytes=mib * 2**20)


def cost(flops, moved, exps=0):
    return pl.CostEstimate(flops=flops // 16, bytes_accessed=moved // 16, transcendentals=exps // 16)


def in_hbm(*arrays):
    return [pltpu.with_memory_space_constraint(a, pltpu.HBM) for a in arrays]


def in_vmem(*arrays):
    return [pltpu.with_memory_space_constraint(a, pltpu.VMEM) for a in arrays]


def weight_cols(which):
    return pl.BlockSpec((D, TILE), lambda t, *_: (which, t))


def weight_rows(which):
    return pl.BlockSpec((TILE, D), lambda t, *_: (which * (D // TILE) + t, 0))


def whole(shape):
    return pl.BlockSpec(shape, lambda t, *_: (0,) * len(shape))


EVEN_PAIRS = [(i, i ^ 1) for i in range(64)]
ODD_PAIRS = [(i, i if i in (0, 63) else ((i + 1) ^ 1) - 1) for i in range(64)]


def exchange(even, odd):
    return lax.ppermute(even, "blk", EVEN_PAIRS), lax.ppermute(odd, "blk", ODD_PAIRS)


def with_parity(kernel, parity, arrays, grid, in_specs, out_specs, out_shape, mib, estimate):
    return pl.pallas_call(
        kernel,
        grid_spec=pltpu.PrefetchScalarGridSpec(
            num_scalar_prefetch=1, grid=grid, in_specs=in_specs, out_specs=out_specs
        ),
        out_shape=out_shape,
        compiler_params=params(mib),
        cost_estimate=estimate,
        name=kernel.__name__,
    )(parity, *arrays)


def halves_of(parity):
    return pl.ds(1 - parity[0], 1), pl.ds(parity[0], 1)


def first_arrays(parity, half_a, half_b, even_ref, odd_ref):
    even_ref[...] = half_a[0]
    odd_ref[...] = half_b[0]


def first_exchange(parity, x):
    shape = (1, BLOCK, D // 2)
    spec = pl.BlockSpec((BLOCK, D // 2), lambda t, p: (0, t))
    return with_parity(
        first_arrays, parity, in_hbm(x, x), (2,),
        [pl.BlockSpec(shape, lambda t, p: (p[0], 0, t)), pl.BlockSpec(shape, lambda t, p: (1 - p[0], 0, t))],
        [spec] * 2, [jax.ShapeDtypeStruct((BLOCK, D), BF)] * 2, 6, cost(0, 8 * BLOCK * D),
    )


def own_kernel(x_ref, wk_ref, wv_ref, kv_ref, wk_out, wv_out):
    wk_out[...] = wk_ref[...]
    wv_out[...] = wv_ref[...]
    x = x_ref[...].reshape(2 * BLOCK, D)
    kv_ref[0] = mm(x, wk_ref[...]).astype(BF).reshape(2, BLOCK, TILE)
    kv_ref[1] = mm(x, wv_ref[...]).astype(BF).reshape(2, BLOCK, TILE)


def own_projections(x, weights):
    return pl.pallas_call(
        own_kernel,
        grid=(D // TILE,),
        in_specs=[whole((2, BLOCK, D)), weight_cols(1), weight_cols(2)],
        out_specs=[pl.BlockSpec((2, 2, BLOCK, TILE), lambda t: (0, 0, 0, t))] + [weight_cols(0)] * 2,
        out_shape=[jax.ShapeDtypeStruct((2, 2, BLOCK, D), BF)] + [jax.ShapeDtypeStruct((D, D), BF)] * 2,
        compiler_params=params(12),
        cost_estimate=cost(8 * 2 * BLOCK * D * D, 12 * D * D + 12 * BLOCK * D),
        name="own_projections",
    )(*in_hbm(x, weights, weights))


def query_kernel(x_ref, g_ref, wq_ref, wo_ref, q_ref, da_ref, wq_out):
    wq_out[...] = wq_ref[...]
    x = x_ref[...].reshape(2 * BLOCK, D)
    g = g_ref[...].reshape(2 * BLOCK, D)
    q_ref[...] = mm(x, wq_ref[...]).astype(BF).reshape(2, BLOCK, TILE)
    da_ref[...] = mm(g, wo_ref[...], NT).astype(BF).reshape(2, BLOCK, TILE)


def query_projections(x, g, weights):
    rows = jax.ShapeDtypeStruct((2, BLOCK, D), BF)
    row_tile = pl.BlockSpec((2, BLOCK, TILE), lambda t: (0, 0, t))
    return pl.pallas_call(
        query_kernel,
        grid=(D // TILE,),
        in_specs=[whole((2, BLOCK, D)), whole((2, BLOCK, D)), weight_cols(0), weight_rows(3)],
        out_specs=[row_tile, row_tile, weight_cols(0)],
        out_shape=[rows, rows, jax.ShapeDtypeStruct((D, D), BF)],
        compiler_params=params(12),
        cost_estimate=cost(8 * 2 * BLOCK * D * D, 12 * D * D + 12 * BLOCK * D),
        name="query_projections",
    )(*in_hbm(x, g, weights, weights))


def halo_projections_kernel(parity, even_ref, odd_ref, wk_ref, wv_ref, kv_ref):
    x = jnp.concatenate([even_ref[...], odd_ref[...]], axis=0)
    for which, w_ref in enumerate((wk_ref, wv_ref)):
        rows = mm(x, w_ref[...]).astype(BF).reshape(2, BLOCK, TILE)
        for i, half in enumerate(halves_of(parity)):
            kv_ref[which, half] = rows[i : i + 1]


def halo_projections(parity, even, odd, wk, wv):
    return with_parity(
        halo_projections_kernel, parity, [even, odd, *in_vmem(wk, wv)], (D // TILE,),
        [whole((BLOCK, D)), whole((BLOCK, D)), weight_cols(0), weight_cols(0)],
        pl.BlockSpec((2, 2, BLOCK, TILE), lambda t, p: (0, 0, 0, t)),
        jax.ShapeDtypeStruct((2, 2, BLOCK, D), BF), 10,
        cost(4 * 2 * BLOCK * D * D, 4 * D * D + 12 * BLOCK * D),
    )


LANES = [slice(i * PAIR, (i + 1) * PAIR) for i in range(PAIRS_A_STEP)]


def first_head():
    return lax.broadcasted_iota(jnp.int32, (BLOCK, PAIR), 1) < HEAD_DIM


def split(rows):
    zero = jnp.zeros_like(rows)
    return jnp.concatenate([jnp.where(first_head(), rows, zero), jnp.where(first_head(), zero, rows)], axis=0)


def merge(rows):
    return jnp.where(first_head(), rows[:BLOCK], rows[BLOCK:])


def stacked(refs, which):
    return [jnp.concatenate([ref[which, 0, :, c] for ref in refs], axis=0) for c in LANES]


def score_limits(block, valid_ref):
    limits = []
    for back in range(WIN - 1, -1, -1):
        key_block = block - back
        slot = jnp.maximum(jnp.where(key_block < 64, key_block, 127 - key_block), 0)
        halves = valid_ref[pl.ds(slot, 1)].reshape(2, BLOCK)
        serves = jnp.where(key_block < 64, halves[:1], halves[1:])
        limit = jnp.where((serves == 1) & (key_block >= 0), FREE, BARRED)
        limits.append(jnp.broadcast_to(limit, (BLOCK, BLOCK)))
    row = lax.broadcasted_iota(jnp.int32, (BLOCK, BLOCK), 0)
    column = lax.broadcasted_iota(jnp.int32, (BLOCK, BLOCK), 1)
    limits[-1] = jnp.where(row == column, FREE, jnp.where(row > column, limits[-1], BARRED))
    bias = jnp.concatenate(limits, axis=1)
    return jnp.concatenate([bias, bias], axis=0)


def attention_out(
    place, valid_ref, q_ref, da_ref, kv3_ref, kv2_ref, kv1_ref, kv0_ref, out_ref, scaled_ref, terms_ref
):
    refs = (kv3_ref, kv2_ref, kv1_ref, kv0_ref)
    bias = score_limits(jnp.where(pl.program_id(0) == 0, place[0], 127 - place[0]), valid_ref)
    ones = jnp.ones((WIN * BLOCK, PAIR), BF)
    keys, values = stacked(refs, 0), stacked(refs, 1)
    scores = [mm(split(q_ref[0, :, c]), k, NT) for c, k in zip(LANES, keys)]
    scores = [jnp.minimum(s, bias) for s in scores]
    tops = [jnp.max(s, axis=1, keepdims=True) for s in scores]
    terms = [jnp.exp2((s - t) * EXP2_SCALE).astype(BF) for s, t in zip(scores, tops)]
    sums = [mm(t, jnp.concatenate([v, ones], axis=1)) for t, v in zip(terms, values)]
    shares = [1.0 / merge(s[:, PAIR:]) for s in sums]
    for i, c in enumerate(LANES):
        out_ref[0, :, c] = (merge(sums[i][:, :PAIR]) * shares[i]).astype(BF)
        scaled_ref[0, :, c] = (da_ref[0, :, c].astype(F32) * shares[i]).astype(BF)
        terms_ref[0, i] = terms[i]


def attention_grads(
    q_ref, kv3_ref, kv2_ref, kv1_ref, kv0_ref, out_ref, scaled_ref, terms_ref,
    dq_ref, d3_ref, d2_ref, d1_ref, d0_ref,
):
    refs = (kv3_ref, kv2_ref, kv1_ref, kv0_ref)
    keys, values = stacked(refs, 0), stacked(refs, 1)
    queries = [split(q_ref[0, :, c]) for c in LANES]
    scaled = [scaled_ref[0, :, c] for c in LANES]
    d_attn = [split(d) for d in scaled]
    terms = [terms_ref[0, i] for i in range(PAIRS_A_STEP)]
    d_probs = [mm(d, v, NT) for d, v in zip(d_attn, values)]
    deltas = [
        jnp.sum(split(d.astype(F32) * out_ref[0, :, c].astype(F32)), axis=1, keepdims=True)
        for c, d in zip(LANES, scaled)
    ]
    d_scores = [(p - d).astype(BF) * t for p, d, t in zip(d_probs, deltas, terms)]
    d_values = [mm(d.T, t).astype(BF).T for d, t in zip(d_attn, terms)]
    d_queries = [merge(mm(d, k)) for d, k in zip(d_scores, keys)]
    for c, d in zip(LANES, d_queries):
        dq_ref[0, :, c] = (d * SCALE).astype(BF)
    d_keys = [(mm(q.T, d) * SCALE).astype(BF).T for q, d in zip(queries, d_scores)]
    for c, dk, dv in zip(LANES, d_keys, d_values):
        for i, ref in enumerate((d3_ref, d2_ref, d1_ref, d0_ref)):
            ref[0, 0, :, c] = dk[i * BLOCK : (i + 1) * BLOCK]
            ref[1, 0, :, c] = dv[i * BLOCK : (i + 1) * BLOCK]


WIDTH = PAIRS_A_STEP * PAIR
ROWS = pl.BlockSpec((1, BLOCK, WIDTH), lambda h, p, *_: (h, 0, p))
PAIRED = pl.BlockSpec((2, 1, BLOCK, WIDTH), lambda h, p, *_: (0, h, 0, p))
VALID = pl.BlockSpec((64, 2, BLOCK), lambda h, p, *_: (0, 0, 0))
TERMS = pl.BlockSpec((1, PAIRS_A_STEP, 2 * BLOCK, WIN * BLOCK), lambda h, p, *_: (h, p, 0, 0))
ROWS_LOW = jax.ShapeDtypeStruct((2, BLOCK, D), BF)
PAIRED_LOW = jax.ShapeDtypeStruct((2, 2, BLOCK, D), BF)
TERMS_LOW = jax.ShapeDtypeStruct((2, HEADS // 2, 2 * BLOCK, WIN * BLOCK), BF)


def attention_forward(place, key_valid, q, da, kvs):
    return with_parity(
        attention_out, place, [key_valid, *in_vmem(q, da, *kvs)], (2, D // WIDTH),
        [VALID, ROWS, ROWS] + [PAIRED] * 4, [ROWS, ROWS, TERMS], [ROWS_LOW, ROWS_LOW, TERMS_LOW], 24,
        cost(2 * 4 * BLOCK * WIN * BLOCK * D * 2, 10 * 2**20, 2**21),
    )


def attention_backward(q, kvs, out, scaled, terms):
    return pl.pallas_call(
        attention_grads,
        grid=(2, D // WIDTH),
        in_specs=[ROWS] + [PAIRED] * 4 + [ROWS, ROWS, TERMS],
        out_specs=[ROWS] + [PAIRED] * 4,
        out_shape=[ROWS_LOW] + [PAIRED_LOW] * 4,
        compiler_params=params(24),
        cost_estimate=cost(2 * 6 * BLOCK * WIN * BLOCK * D * 2, 12 * 2**20),
        name="attention_grads",
    )(*in_vmem(q, *kvs, out, scaled, terms))


def in_order(parity, ref, *lead):
    return jnp.concatenate([ref[(*lead, half)] for half in halves_of(parity)], axis=0).reshape(2 * BLOCK, D)


def back_projections_kernel(parity, d_ref, wk_ref, wv_ref, even_ref, odd_ref):
    rows = mm(in_order(parity, d_ref, 0), wk_ref[...], NT)
    rows += mm(in_order(parity, d_ref, 1), wv_ref[...], NT)
    even_ref[...] = rows[:BLOCK].astype(BF)
    odd_ref[...] = rows[BLOCK:].astype(BF)


def last_projections_kernel(parity, d_ref, dq_ref, wq_ref, wk_ref, wv_ref, even_ref, odd_ref):
    rows = mm(in_order(parity, dq_ref), wq_ref[...], NT)
    rows += mm(in_order(parity, d_ref, 0), wk_ref[...], NT)
    rows += mm(in_order(parity, d_ref, 1), wv_ref[...], NT)
    even_ref[...] = rows[:BLOCK]
    odd_ref[...] = rows[BLOCK:]


def back_projections(parity, d, wk, wv):
    return with_parity(
        back_projections_kernel, parity, in_vmem(d, wk, wv), (D // TILE,),
        [whole((2, 2, BLOCK, D)), weight_rows(0), weight_rows(0)],
        [pl.BlockSpec((BLOCK, TILE), lambda t, p: (0, t))] * 2,
        [jax.ShapeDtypeStruct((BLOCK, D), BF)] * 2, 10,
        cost(4 * 2 * BLOCK * D * D, 4 * D * D + 12 * BLOCK * D),
    )


def last_projections(parity, d, dq, wq, wk, wv):
    return with_parity(
        last_projections_kernel, parity, in_vmem(d, dq, wq, wk, wv), (D // TILE,),
        [whole((2, 2, BLOCK, D)), whole((2, BLOCK, D)), weight_rows(0), weight_rows(0), weight_rows(0)],
        [pl.BlockSpec((BLOCK, TILE), lambda t, p: (0, t))] * 2,
        [jax.ShapeDtypeStruct((BLOCK, D), F32)] * 2, 12,
        cost(6 * 2 * BLOCK * D * D, 6 * D * D + 16 * BLOCK * D),
    )


def outer_kernel(core_ref, o_ref, keep_ref, send_ref, kept_ref, sent_ref):
    o_t = o_ref[...].reshape(2 * BLOCK, D).T
    for g_ref, r_ref in ((send_ref, sent_ref), (keep_ref, kept_ref)):
        r_ref[0] = mm(o_t, g_ref[...].reshape(2 * BLOCK, TILE)).astype(BF)


def outer_products(o, g, core):
    result = jax.ShapeDtypeStruct((2, D, TILE), BF)
    result_spec = pl.BlockSpec((1, D, TILE), lambda y, c: (y, 0, 0))
    return pl.pallas_call(
        outer_kernel,
        grid_spec=pltpu.PrefetchScalarGridSpec(
            num_scalar_prefetch=1,
            grid=(2,),
            in_specs=[
                pl.BlockSpec((2, BLOCK, D), lambda y, c: (0, 0, 0)),
                pl.BlockSpec((2, BLOCK, TILE), lambda y, c: (0, 0, 2 * y + c[0])),
                pl.BlockSpec((2, BLOCK, TILE), lambda y, c: (0, 0, 2 * y + 1 - c[0])),
            ],
            out_specs=[result_spec, result_spec],
        ),
        out_shape=[result, result],
        compiler_params=params(12),
        cost_estimate=cost(4 * BLOCK * D * D, 2 * D * D + 8 * BLOCK * D),
        name="outer_products",
    )(core, *in_vmem(o, g, g))


def hop_sums(even_ref, odd_ref, from_even, from_odd):
    return (
        (even_ref[...].astype(F32) + from_odd[...].astype(F32)).astype(BF),
        (odd_ref[...].astype(F32) + from_even[...].astype(F32)).astype(BF),
    )


def hop_kernel(parity, even_ref, odd_ref, from_even, from_odd, even_out, odd_out):
    even_out[...], odd_out[...] = hop_sums(even_ref, odd_ref, from_even, from_odd)


def final_kernel(parity, even_ref, odd_ref, from_even, from_odd, out_ref):
    for half, rows in zip(halves_of(parity), hop_sums(even_ref, odd_ref, from_even, from_odd)):
        out_ref[half] = rows[None]


def hop_back(parity, terms, moved, last=False):
    spec = pl.BlockSpec((BLOCK, D // 2), lambda t, p: (0, t))
    if last:
        out_specs = pl.BlockSpec((2, BLOCK, D // 2), lambda t, p: (0, 0, t))
        out_shape = jax.ShapeDtypeStruct((2, BLOCK, D), BF)
    else:
        out_specs = [spec] * 2
        out_shape = [jax.ShapeDtypeStruct((BLOCK, D), BF)] * 2
    return with_parity(
        final_kernel if last else hop_kernel, parity, in_vmem(*terms, *moved), (2,),
        [spec] * 4, out_specs, out_shape, 6, cost(8 * BLOCK * D, 14 * BLOCK * D),
    )


def chip(y, x, z, core):
    return ((y % 2) * 32 + x * 8 + z) * 4 + (y // 2) * 2 + core


CORE_PAIRS = [(i, i ^ 1) for i in range(4)]
LINES = [[32 * y + 8 * x + z for z in range(8)] for y in range(2) for x in range(4)]
FLIP = ((1, 0, 3, 2), (3, 2, 1, 0))


def halving_pairs(second, turn):
    pairs = []
    for y in range(4):
        for x in range(4):
            for z in range(8):
                for core in range(2):
                    along_x = (core == 0) != second
                    to = (y, FLIP[turn][x]) if along_x else (FLIP[turn][y], x)
                    pairs.append((chip(y, x, z, core), chip(*to, z, core)))
    return pairs


SHARE = 128


def places(position, shot):
    def ring(i):
        outer = (i == 0) | (i == 3)
        keep = [jnp.where(outer, 0, 1), jnp.where(outer, 3, 2)]
        send = [jnp.where(outer, 1, 0), jnp.where(outer, 2, 3)]
        return keep + send + [i // 2, 1 - i // 2]

    core = shot % 2
    x = (position // 8) % 4
    y = (shot // 2) * 2 + position // 32
    first, second = jnp.where(core == 0, x, y), jnp.where(core == 0, y, x)
    return jnp.stack([position, core] + ring(first) + ring(second)).astype(jnp.int32)


FIRST, SECOND = 2, 8


def total(a, b):
    return (a.astype(F32) + b.astype(F32)).astype(BF)


def split_core(place, kept_ref, other_ref, keep_ref, send_ref):
    for out_ref, at in ((keep_ref, FIRST), (send_ref, FIRST + 2)):
        for i in range(2):
            for j in range(4):
                first = place[at + i]
                y = pl.ds(jnp.where(place[1] == 0, j, first), 1)
                x = pl.ds(jnp.where(place[1] == 0, first, j), 1)
                out_ref[i : i + 1, j : j + 1] = total(kept_ref[y, x], other_ref[y, x])


def split_first(place, kept_ref, moved_ref, keep_ref, send_ref):
    for j, out_ref in enumerate((keep_ref, send_ref)):
        i = pl.ds(place[FIRST + 4 + j], 1)
        out_ref[...] = total(kept_ref[i], moved_ref[i])


def split_second(place, kept_ref, moved_ref, keep_ref, send_ref):
    for out_ref, at in ((keep_ref, SECOND), (send_ref, SECOND + 2)):
        for j in range(2):
            i = pl.ds(place[at + j], 1)
            out_ref[:, j : j + 1] = total(kept_ref[:, i], moved_ref[:, i])


def split_third(place, kept_ref, moved_ref, keep_ref, send_ref):
    for j, out_ref in enumerate((keep_ref, send_ref)):
        i = pl.ds(place[SECOND + 4 + j], 1)
        out_ref[...] = total(kept_ref[:, i], moved_ref[:, i])


def join_last(place, kept_ref, moved_ref, out_ref):
    out_ref[...] = total(kept_ref[...], moved_ref[...])


def halving(kernel, place, arrays, shapes):
    vmem = pl.BlockSpec(memory_space=pltpu.VMEM)
    return pl.pallas_call(
        kernel,
        in_specs=[pl.BlockSpec(memory_space=pltpu.SMEM)] + [vmem] * len(arrays),
        out_specs=[vmem] * len(shapes),
        out_shape=[jax.ShapeDtypeStruct(shape + (SHARE, TILE), BF) for shape in shapes],
        compiler_params=params(8),
        cost_estimate=cost(2**20, 2**20),
        name=kernel.__name__,
    )(place, *arrays)


def halve_core(place, kept, other):
    arrays = [v.reshape(4, 4, SHARE, TILE) for v in (kept, other)]
    return halving(split_core, place, arrays, [(2, 4)] * 2)


HALVINGS = (
    (split_first, halving_pairs(False, 0), [(1, 4)] * 2),
    (split_second, halving_pairs(False, 1), [(1, 2)] * 2),
    (split_third, halving_pairs(True, 0), [(1, 1)] * 2),
    (join_last, halving_pairs(True, 1), [(1, 1)]),
)


def after(values, ready):
    return lax.optimization_barrier((values, ready))[0]


def halve(turn, place, pieces, ready):
    kernel, pairs, shapes = HALVINGS[turn]
    keep, send = pieces
    moved = after(lax.ppermute(send, ("blk", "dp"), pairs), ready)
    return halving(kernel, place, [keep, moved], shapes)


def sum_over_line(total):
    total = lax.all_to_all(total.reshape(8, 16, TILE), "blk", 0, 0, axis_index_groups=LINES)
    return jnp.sum(total.astype(F32), axis=0)


def per_device(tokens, key_valid, weights, out_grad):
    position = lax.axis_index("blk")
    shot = lax.axis_index("dp")
    x = tokens.reshape(2, BLOCK, D)
    g = out_grad.reshape(2, BLOCK, D)

    parity = (position % 2).reshape(1)
    state = first_exchange(parity, x)
    core = (shot % 2).reshape(1)
    place = places(position, shot)
    own, core, place = lax.optimization_barrier((x, core, place))
    kv0, wk, wv = own_projections(own, weights)
    kvs = [kv0]
    for hop_index in range(WIN - 1):
        from_even, from_odd = exchange(*state)
        if hop_index == 1:
            q, da, wq, kvs[-1] = lax.optimization_barrier((*query_projections(own, g, weights), kvs[-1]))
            from_even, from_odd, q = lax.optimization_barrier((from_even, from_odd, q))
        from_even, from_odd, kvs[-1] = lax.optimization_barrier((from_even, from_odd, kvs[-1]))
        kvs.append(halo_projections(parity, from_even, from_odd, wk, wv))
        state = from_odd, from_even
    kvs = kvs[::-1]
    o, scaled, exps = attention_forward(place, key_valid.reshape(64, 2, BLOCK), q, da, kvs)

    kept, sent = outer_products(o, g, core)
    pieces = halve_core(place, kept, lax.ppermute(sent, "dp", CORE_PAIRS))
    exps, pieces = lax.optimization_barrier((exps, pieces))
    dq, d3, d2, d1, d0 = attention_backward(q, kvs, o, scaled, exps)
    state = back_projections(parity, d3, wk, wv)

    moved = exchange(*state)
    d2, d1, state = lax.optimization_barrier((d2, d1, state))
    terms = back_projections(parity, d2, wk, wv)
    later = back_projections(parity, d1, wk, wv)
    pieces = halve(1, place, halve(0, place, pieces, terms), later)
    pieces = halve(2, place, pieces, pieces)
    state = hop_back(parity, terms, after(moved, pieces))

    moved = exchange(*state)
    last = last_projections(parity, after(d0, state), dq, wq, wk, wv)
    (plane_sum,) = halve(3, place, pieces, last)
    state = hop_back(parity, later, after(moved, plane_sum))

    moved = exchange(*state)
    grad_tokens = hop_back(parity, last, moved, True)
    w_grad = sum_over_line(plane_sum)
    return grad_tokens.reshape(tokens.shape), w_grad


def solution(mesh):
    placed = (
        P("dp", "blk", None, None, None),
        P("dp", None, None, None),
        P(),
        P("dp", "blk", None, None, None),
    )
    return jax.shard_map(
        per_device,
        mesh=mesh,
        in_specs=placed,
        out_specs=(P("dp", "blk", None, None, None), P("blk", "dp")),
        check_vma=False,
    )
```

```python
import jax
import jax.numpy as jnp
import numpy as np
from jax import lax
from jax.experimental import pallas as pl
from jax.experimental.pallas import tpu as pltpu
from jax.sharding import PartitionSpec as P

HEADS = 16
HEAD_DIM = 64
WIN = 4
BLOCK = 128
D = 1024
PAIR = 2 * HEAD_DIM
PAIRS_A_STEP = 4
TILE = 256
BF = jnp.bfloat16
F32 = jnp.float32

BARRED = -1e30
FREE = 3e38
SCALE = HEAD_DIM**-0.5
EXP2_SCALE = float(SCALE * np.log2(np.e))

NN = (((1,), (0,)), ((), ()))
NT = (((1,), (1,)), ((), ()))


def mm(a, b, dims=NN):
    return lax.dot_general(a, b, dims, preferred_element_type=F32)


def params(mib):
    return pltpu.CompilerParams(vmem_limit_bytes=mib * 2**20)


def cost(flops, moved, exps=0):
    return pl.CostEstimate(flops=flops // 16, bytes_accessed=moved // 16, transcendentals=exps // 16)


def in_hbm(*arrays):
    return [pltpu.with_memory_space_constraint(a, pltpu.HBM) for a in arrays]


def in_vmem(*arrays):
    return [pltpu.with_memory_space_constraint(a, pltpu.VMEM) for a in arrays]


def weight_cols(which):
    return pl.BlockSpec((D, TILE), lambda t, *_: (which, t))


def weight_rows(which):
    return pl.BlockSpec((TILE, D), lambda t, *_: (which * (D // TILE) + t, 0))


def whole(shape):
    return pl.BlockSpec(shape, lambda t, *_: (0,) * len(shape))


EVEN_PAIRS = [(i, i ^ 1) for i in range(64)]
ODD_PAIRS = [(i, i if i in (0, 63) else ((i + 1) ^ 1) - 1) for i in range(64)]


def exchange(even, odd):
    return lax.ppermute(even, "blk", EVEN_PAIRS), lax.ppermute(odd, "blk", ODD_PAIRS)


def with_parity(kernel, parity, arrays, grid, in_specs, out_specs, out_shape, mib, estimate):
    return pl.pallas_call(
        kernel,
        grid_spec=pltpu.PrefetchScalarGridSpec(
            num_scalar_prefetch=1, grid=grid, in_specs=in_specs, out_specs=out_specs
        ),
        out_shape=out_shape,
        compiler_params=params(mib),
        cost_estimate=estimate,
        name=kernel.__name__,
    )(parity, *arrays)


def halves_of(parity):
    return pl.ds(1 - parity[0], 1), pl.ds(parity[0], 1)


def first_arrays(parity, half_a, half_b, even_ref, odd_ref):
    even_ref[...] = half_a[0]
    odd_ref[...] = half_b[0]


def first_exchange(parity, x):
    shape = (1, BLOCK, D // 2)
    spec = pl.BlockSpec((BLOCK, D // 2), lambda t, p: (0, t))
    return with_parity(
        first_arrays, parity, in_hbm(x, x), (2,),
        [pl.BlockSpec(shape, lambda t, p: (p[0], 0, t)), pl.BlockSpec(shape, lambda t, p: (1 - p[0], 0, t))],
        [spec] * 2, [jax.ShapeDtypeStruct((BLOCK, D), BF)] * 2, 6, cost(0, 8 * BLOCK * D),
    )


def own_kernel(x_ref, wk_ref, wv_ref, kv_ref, wk_out, wv_out):
    wk_out[...] = wk_ref[...]
    wv_out[...] = wv_ref[...]
    x = x_ref[...].reshape(2 * BLOCK, D)
    kv_ref[0] = mm(x, wk_ref[...]).astype(BF).reshape(2, BLOCK, TILE)
    kv_ref[1] = mm(x, wv_ref[...]).astype(BF).reshape(2, BLOCK, TILE)


def own_projections(x, weights):
    return pl.pallas_call(
        own_kernel,
        grid=(D // TILE,),
        in_specs=[whole((2, BLOCK, D)), weight_cols(1), weight_cols(2)],
        out_specs=[pl.BlockSpec((2, 2, BLOCK, TILE), lambda t: (0, 0, 0, t))] + [weight_cols(0)] * 2,
        out_shape=[jax.ShapeDtypeStruct((2, 2, BLOCK, D), BF)] + [jax.ShapeDtypeStruct((D, D), BF)] * 2,
        compiler_params=params(12),
        cost_estimate=cost(8 * 2 * BLOCK * D * D, 12 * D * D + 12 * BLOCK * D),
        name="own_projections",
    )(*in_hbm(x, weights, weights))


def query_kernel(x_ref, g_ref, wq_ref, wo_ref, q_ref, da_ref, wq_out):
    wq_out[...] = wq_ref[...]
    x = x_ref[...].reshape(2 * BLOCK, D)
    g = g_ref[...].reshape(2 * BLOCK, D)
    q_ref[...] = mm(x, wq_ref[...]).astype(BF).reshape(2, BLOCK, TILE)
    da_ref[...] = mm(g, wo_ref[...], NT).astype(BF).reshape(2, BLOCK, TILE)


def query_projections(x, g, weights):
    rows = jax.ShapeDtypeStruct((2, BLOCK, D), BF)
    row_tile = pl.BlockSpec((2, BLOCK, TILE), lambda t: (0, 0, t))
    return pl.pallas_call(
        query_kernel,
        grid=(D // TILE,),
        in_specs=[whole((2, BLOCK, D)), whole((2, BLOCK, D)), weight_cols(0), weight_rows(3)],
        out_specs=[row_tile, row_tile, weight_cols(0)],
        out_shape=[rows, rows, jax.ShapeDtypeStruct((D, D), BF)],
        compiler_params=params(12),
        cost_estimate=cost(8 * 2 * BLOCK * D * D, 12 * D * D + 12 * BLOCK * D),
        name="query_projections",
    )(*in_hbm(x, g, weights, weights))


def halo_projections_kernel(parity, even_ref, odd_ref, wk_ref, wv_ref, kv_ref):
    x = jnp.concatenate([even_ref[...], odd_ref[...]], axis=0)
    for which, w_ref in enumerate((wk_ref, wv_ref)):
        rows = mm(x, w_ref[...]).astype(BF).reshape(2, BLOCK, TILE)
        for i, half in enumerate(halves_of(parity)):
            kv_ref[which, half] = rows[i : i + 1]


def halo_projections(parity, even, odd, wk, wv):
    return with_parity(
        halo_projections_kernel, parity, [even, odd, *in_vmem(wk, wv)], (D // TILE,),
        [whole((BLOCK, D)), whole((BLOCK, D)), weight_cols(0), weight_cols(0)],
        pl.BlockSpec((2, 2, BLOCK, TILE), lambda t, p: (0, 0, 0, t)),
        jax.ShapeDtypeStruct((2, 2, BLOCK, D), BF), 10,
        cost(4 * 2 * BLOCK * D * D, 4 * D * D + 12 * BLOCK * D),
    )


LANES = [slice(i * PAIR, (i + 1) * PAIR) for i in range(PAIRS_A_STEP)]


def first_head():
    return lax.broadcasted_iota(jnp.int32, (BLOCK, PAIR), 1) < HEAD_DIM


def split(rows):
    zero = jnp.zeros_like(rows)
    return jnp.concatenate([jnp.where(first_head(), rows, zero), jnp.where(first_head(), zero, rows)], axis=0)


def merge(rows):
    return jnp.where(first_head(), rows[:BLOCK], rows[BLOCK:])


def stacked(refs, which):
    return [jnp.concatenate([ref[which, 0, :, c] for ref in refs], axis=0) for c in LANES]


def score_limits(block, valid_ref):
    limits = []
    for back in range(WIN - 1, -1, -1):
        key_block = block - back
        slot = jnp.maximum(jnp.where(key_block < 64, key_block, 127 - key_block), 0)
        halves = valid_ref[pl.ds(slot, 1)].reshape(2, BLOCK)
        serves = jnp.where(key_block < 64, halves[:1], halves[1:])
        limit = jnp.where((serves == 1) & (key_block >= 0), FREE, BARRED)
        limits.append(jnp.broadcast_to(limit, (BLOCK, BLOCK)))
    row = lax.broadcasted_iota(jnp.int32, (BLOCK, BLOCK), 0)
    column = lax.broadcasted_iota(jnp.int32, (BLOCK, BLOCK), 1)
    limits[-1] = jnp.where(row == column, FREE, jnp.where(row > column, limits[-1], BARRED))
    bias = jnp.concatenate(limits, axis=1)
    return jnp.concatenate([bias, bias], axis=0)


def attention_out(
    place, valid_ref, q_ref, da_ref, kv3_ref, kv2_ref, kv1_ref, kv0_ref, out_ref, scaled_ref, terms_ref
):
    refs = (kv3_ref, kv2_ref, kv1_ref, kv0_ref)
    bias = score_limits(jnp.where(pl.program_id(0) == 0, place[0], 127 - place[0]), valid_ref)
    ones = jnp.ones((WIN * BLOCK, PAIR), BF)
    keys, values = stacked(refs, 0), stacked(refs, 1)
    scores = [mm(split(q_ref[0, :, c]), k, NT) for c, k in zip(LANES, keys)]
    scores = [jnp.minimum(s, bias) for s in scores]
    tops = [jnp.max(s, axis=1, keepdims=True) for s in scores]
    terms = [jnp.exp2((s - t) * EXP2_SCALE).astype(BF) for s, t in zip(scores, tops)]
    sums = [mm(t, jnp.concatenate([v, ones], axis=1)) for t, v in zip(terms, values)]
    shares = [1.0 / merge(s[:, PAIR:]) for s in sums]
    for i, c in enumerate(LANES):
        out_ref[0, :, c] = (merge(sums[i][:, :PAIR]) * shares[i]).astype(BF)
        scaled_ref[0, :, c] = (da_ref[0, :, c].astype(F32) * shares[i]).astype(BF)
        terms_ref[0, i] = terms[i]


def attention_grads(
    q_ref, kv3_ref, kv2_ref, kv1_ref, kv0_ref, out_ref, scaled_ref, terms_ref,
    dq_ref, d3_ref, d2_ref, d1_ref, d0_ref,
):
    refs = (kv3_ref, kv2_ref, kv1_ref, kv0_ref)
    keys, values = stacked(refs, 0), stacked(refs, 1)
    queries = [split(q_ref[0, :, c]) for c in LANES]
    scaled = [scaled_ref[0, :, c] for c in LANES]
    d_attn = [split(d) for d in scaled]
    terms = [terms_ref[0, i] for i in range(PAIRS_A_STEP)]
    d_probs = [mm(d, v, NT) for d, v in zip(d_attn, values)]
    deltas = [
        jnp.sum(split(d.astype(F32) * out_ref[0, :, c].astype(F32)), axis=1, keepdims=True)
        for c, d in zip(LANES, scaled)
    ]
    d_scores = [(p - d).astype(BF) * t for p, d, t in zip(d_probs, deltas, terms)]
    d_values = [mm(d.T, t).astype(BF).T for d, t in zip(d_attn, terms)]
    d_queries = [merge(mm(d, k)) for d, k in zip(d_scores, keys)]
    for c, d in zip(LANES, d_queries):
        dq_ref[0, :, c] = (d * SCALE).astype(BF)
    d_keys = [(mm(q.T, d) * SCALE).astype(BF).T for q, d in zip(queries, d_scores)]
    for c, dk, dv in zip(LANES, d_keys, d_values):
        for i, ref in enumerate((d3_ref, d2_ref, d1_ref, d0_ref)):
            ref[0, 0, :, c] = dk[i * BLOCK : (i + 1) * BLOCK]
            ref[1, 0, :, c] = dv[i * BLOCK : (i + 1) * BLOCK]


WIDTH = PAIRS_A_STEP * PAIR
ROWS = pl.BlockSpec((1, BLOCK, WIDTH), lambda h, p, *_: (h, 0, p))
PAIRED = pl.BlockSpec((2, 1, BLOCK, WIDTH), lambda h, p, *_: (0, h, 0, p))
VALID = pl.BlockSpec((64, 2, BLOCK), lambda h, p, *_: (0, 0, 0))
TERMS = pl.BlockSpec((1, PAIRS_A_STEP, 2 * BLOCK, WIN * BLOCK), lambda h, p, *_: (h, p, 0, 0))
ROWS_LOW = jax.ShapeDtypeStruct((2, BLOCK, D), BF)
PAIRED_LOW = jax.ShapeDtypeStruct((2, 2, BLOCK, D), BF)
TERMS_LOW = jax.ShapeDtypeStruct((2, HEADS // 2, 2 * BLOCK, WIN * BLOCK), BF)


def attention_forward(place, key_valid, q, da, kvs):
    return with_parity(
        attention_out, place, [key_valid, *in_vmem(q, da, *kvs)], (2, D // WIDTH),
        [VALID, ROWS, ROWS] + [PAIRED] * 4, [ROWS, ROWS, TERMS], [ROWS_LOW, ROWS_LOW, TERMS_LOW], 24,
        cost(2 * 4 * BLOCK * WIN * BLOCK * D * 2, 10 * 2**20, 2**21),
    )


def attention_backward(half, q, kvs, out, scaled, terms, so_far=()):
    rows = pl.BlockSpec((1, BLOCK, WIDTH), lambda p: (half, 0, p))
    paired = pl.BlockSpec((2, 1, BLOCK, WIDTH), lambda p: (0, half, 0, p))
    held = pl.BlockSpec((1, PAIRS_A_STEP, 2 * BLOCK, WIN * BLOCK), lambda p: (half, p, 0, 0))

    def kernel(*refs):
        attention_grads(*refs[:8], *refs[8 + len(so_far) :])

    return pl.pallas_call(
        kernel,
        grid=(D // WIDTH,),
        in_specs=[rows] + [paired] * 4 + [rows, rows, held] + [pl.BlockSpec(memory_space=pl.ANY)] * len(so_far),
        out_specs=[rows] + [paired] * 4,
        out_shape=[ROWS_LOW] + [PAIRED_LOW] * 4,
        input_output_aliases={8 + i: i for i in range(len(so_far))},
        compiler_params=params(24),
        cost_estimate=cost(6 * BLOCK * WIN * BLOCK * D * 2, 6 * 2**20),
        name="attention_grads",
    )(*in_vmem(q, *kvs, out, scaled, terms), *so_far)


def in_order(parity, ref, *lead):
    return jnp.concatenate([ref[(*lead, half)] for half in halves_of(parity)], axis=0).reshape(2 * BLOCK, D)


def back_projections_kernel(parity, d_ref, wk_ref, wv_ref, even_ref, odd_ref):
    rows = mm(in_order(parity, d_ref, 0), wk_ref[...], NT)
    rows += mm(in_order(parity, d_ref, 1), wv_ref[...], NT)
    even_ref[...] = rows[:BLOCK].astype(BF)
    odd_ref[...] = rows[BLOCK:].astype(BF)


def last_projections_kernel(parity, d_ref, dq_ref, wq_ref, wk_ref, wv_ref, even_ref, odd_ref):
    rows = mm(in_order(parity, dq_ref), wq_ref[...], NT)
    rows += mm(in_order(parity, d_ref, 0), wk_ref[...], NT)
    rows += mm(in_order(parity, d_ref, 1), wv_ref[...], NT)
    even_ref[...] = rows[:BLOCK]
    odd_ref[...] = rows[BLOCK:]


def back_projections(parity, d, wk, wv):
    return with_parity(
        back_projections_kernel, parity, in_vmem(d, wk, wv), (D // TILE,),
        [whole((2, 2, BLOCK, D)), weight_rows(0), weight_rows(0)],
        [pl.BlockSpec((BLOCK, TILE), lambda t, p: (0, t))] * 2,
        [jax.ShapeDtypeStruct((BLOCK, D), BF)] * 2, 10,
        cost(4 * 2 * BLOCK * D * D, 4 * D * D + 12 * BLOCK * D),
    )


def last_projections(parity, d, dq, wq, wk, wv):
    return with_parity(
        last_projections_kernel, parity, in_vmem(d, dq, wq, wk, wv), (D // TILE,),
        [whole((2, 2, BLOCK, D)), whole((2, BLOCK, D)), weight_rows(0), weight_rows(0), weight_rows(0)],
        [pl.BlockSpec((BLOCK, TILE), lambda t, p: (0, t))] * 2,
        [jax.ShapeDtypeStruct((BLOCK, D), F32)] * 2, 12,
        cost(6 * 2 * BLOCK * D * D, 6 * D * D + 16 * BLOCK * D),
    )


def outer_kernel(core_ref, o_ref, keep_ref, send_ref, kept_ref, sent_ref):
    o_t = o_ref[...].reshape(2 * BLOCK, D).T
    for g_ref, r_ref in ((send_ref, sent_ref), (keep_ref, kept_ref)):
        r_ref[0] = mm(o_t, g_ref[...].reshape(2 * BLOCK, TILE)).astype(BF)


def outer_products(o, g, core):
    result = jax.ShapeDtypeStruct((2, D, TILE), BF)
    result_spec = pl.BlockSpec((1, D, TILE), lambda y, c: (y, 0, 0))
    return pl.pallas_call(
        outer_kernel,
        grid_spec=pltpu.PrefetchScalarGridSpec(
            num_scalar_prefetch=1,
            grid=(2,),
            in_specs=[
                pl.BlockSpec((2, BLOCK, D), lambda y, c: (0, 0, 0)),
                pl.BlockSpec((2, BLOCK, TILE), lambda y, c: (0, 0, 2 * y + c[0])),
                pl.BlockSpec((2, BLOCK, TILE), lambda y, c: (0, 0, 2 * y + 1 - c[0])),
            ],
            out_specs=[result_spec, result_spec],
        ),
        out_shape=[result, result],
        compiler_params=params(12),
        cost_estimate=cost(4 * BLOCK * D * D, 2 * D * D + 8 * BLOCK * D),
        name="outer_products",
    )(core, *in_vmem(o, g, g))


def hop_sums(even_ref, odd_ref, from_even, from_odd):
    return (
        (even_ref[...].astype(F32) + from_odd[...].astype(F32)).astype(BF),
        (odd_ref[...].astype(F32) + from_even[...].astype(F32)).astype(BF),
    )


def hop_kernel(term_ref, moved_ref, out_ref):
    out_ref[...] = (term_ref[...].astype(F32) + moved_ref[...].astype(F32)).astype(BF)


def final_kernel(parity, even_ref, odd_ref, from_even, from_odd, out_ref):
    for half, rows in zip(halves_of(parity), hop_sums(even_ref, odd_ref, from_even, from_odd)):
        out_ref[half] = rows[None]


def hop_back(term, moved):
    spec = pl.BlockSpec((BLOCK, D // 2), lambda t: (0, t))
    return pl.pallas_call(
        hop_kernel,
        grid=(2,),
        in_specs=[spec] * 2,
        out_specs=spec,
        out_shape=jax.ShapeDtypeStruct((BLOCK, D), BF),
        compiler_params=params(6),
        cost_estimate=cost(4 * BLOCK * D, 6 * BLOCK * D),
        name="hop_back",
    )(*in_vmem(term, moved))


def final_hop(parity, terms, moved):
    spec = pl.BlockSpec((BLOCK, D // 2), lambda t, p: (0, t))
    return with_parity(
        final_kernel, parity, in_vmem(*terms, *moved), (2,), [spec] * 4,
        pl.BlockSpec((2, BLOCK, D // 2), lambda t, p: (0, 0, t)),
        jax.ShapeDtypeStruct((2, BLOCK, D), BF), 6, cost(8 * BLOCK * D, 14 * BLOCK * D),
    )


def chip(y, x, z, core):
    return ((y % 2) * 32 + x * 8 + z) * 4 + (y // 2) * 2 + core


CORE_PAIRS = [(i, i ^ 1) for i in range(4)]
LINES = [[32 * y + 8 * x + z for z in range(8)] for y in range(2) for x in range(4)]
FLIP = ((1, 0, 3, 2), (3, 2, 1, 0))


def halving_pairs(second, turn):
    pairs = []
    for y in range(4):
        for x in range(4):
            for z in range(8):
                for core in range(2):
                    along_x = (core == 0) != second
                    to = (y, FLIP[turn][x]) if along_x else (FLIP[turn][y], x)
                    pairs.append((chip(y, x, z, core), chip(*to, z, core)))
    return pairs


SHARE = 128


def places(position, shot):
    def ring(i):
        outer = (i == 0) | (i == 3)
        keep = [jnp.where(outer, 0, 1), jnp.where(outer, 3, 2)]
        send = [jnp.where(outer, 1, 0), jnp.where(outer, 2, 3)]
        return keep + send + [i // 2, 1 - i // 2]

    core = shot % 2
    x = (position // 8) % 4
    y = (shot // 2) * 2 + position // 32
    first, second = jnp.where(core == 0, x, y), jnp.where(core == 0, y, x)
    return jnp.stack([position, core] + ring(first) + ring(second)).astype(jnp.int32)


FIRST, SECOND = 2, 8


def total(a, b):
    return (a.astype(F32) + b.astype(F32)).astype(BF)


def split_core(place, kept_ref, other_ref, keep_ref, send_ref):
    for out_ref, at in ((keep_ref, FIRST), (send_ref, FIRST + 2)):
        for i in range(2):
            for j in range(4):
                first = place[at + i]
                y = pl.ds(jnp.where(place[1] == 0, j, first), 1)
                x = pl.ds(jnp.where(place[1] == 0, first, j), 1)
                out_ref[i : i + 1, j : j + 1] = total(kept_ref[y, x], other_ref[y, x])


def split_first(place, kept_ref, moved_ref, keep_ref, send_ref):
    for j, out_ref in enumerate((keep_ref, send_ref)):
        i = pl.ds(place[FIRST + 4 + j], 1)
        out_ref[...] = total(kept_ref[i], moved_ref[i])


def split_second(place, kept_ref, moved_ref, keep_ref, send_ref):
    for out_ref, at in ((keep_ref, SECOND), (send_ref, SECOND + 2)):
        for j in range(2):
            i = pl.ds(place[at + j], 1)
            out_ref[:, j : j + 1] = total(kept_ref[:, i], moved_ref[:, i])


def split_third(place, kept_ref, moved_ref, keep_ref, send_ref):
    for j, out_ref in enumerate((keep_ref, send_ref)):
        i = pl.ds(place[SECOND + 4 + j], 1)
        out_ref[...] = total(kept_ref[:, i], moved_ref[:, i])


def join_last(place, kept_ref, moved_ref, out_ref):
    out_ref[...] = total(kept_ref[...], moved_ref[...])


def halving(kernel, place, arrays, shapes, ready=()):
    vmem = pl.BlockSpec(memory_space=pltpu.VMEM)
    count = 1 + len(arrays)

    def body(*refs):
        kernel(*refs[:count], *refs[count + len(ready) :])

    return pl.pallas_call(
        body,
        in_specs=[pl.BlockSpec(memory_space=pltpu.SMEM)]
        + [vmem] * len(arrays)
        + [pl.BlockSpec(memory_space=pl.ANY)] * len(ready),
        out_specs=[vmem] * len(shapes),
        out_shape=[jax.ShapeDtypeStruct(shape + (SHARE, TILE), BF) for shape in shapes],
        compiler_params=params(8),
        cost_estimate=cost(2**20, 2**20),
        name=kernel.__name__,
    )(place, *arrays, *ready)


def halve_core(place, kept, other):
    arrays = [v.reshape(4, 4, SHARE, TILE) for v in (kept, other)]
    return halving(split_core, place, arrays, [(2, 4)] * 2)


HALVINGS = (
    (split_first, halving_pairs(False, 0), [(1, 4)] * 2),
    (split_second, halving_pairs(False, 1), [(1, 2)] * 2),
    (split_third, halving_pairs(True, 0), [(1, 1)] * 2),
    (join_last, halving_pairs(True, 1), [(1, 1)]),
)


together = lax.optimization_barrier


def send_pieces(turn, pieces):
    return lax.ppermute(pieces[1], ("blk", "dp"), HALVINGS[turn][1])


def halve(turn, place, pieces, moved, ready=()):
    kernel, _, shapes = HALVINGS[turn]
    return halving(kernel, place, [pieces[0], moved], shapes, ready)


def sum_over_line(total, ready):
    total = lax.all_to_all(total.reshape(8, 16, TILE), "blk", 0, 0, axis_index_groups=LINES)
    return jnp.sum(together((total, ready))[0].astype(F32), axis=0)


def per_device(tokens, key_valid, weights, out_grad):
    position = lax.axis_index("blk")
    shot = lax.axis_index("dp")
    x = tokens.reshape(2, BLOCK, D)
    g = out_grad.reshape(2, BLOCK, D)

    parity = (position % 2).reshape(1)
    state = first_exchange(parity, x)
    core = (shot % 2).reshape(1)
    place = places(position, shot)
    own, core, place = lax.optimization_barrier((x, core, place))
    kv0, wk, wv = own_projections(own, weights)
    even, odd = exchange(*state)
    even, kv0 = together((even, kv0))
    even_2, odd_2 = exchange(odd, even)
    kv1 = halo_projections(parity, even, odd, wk, wv)
    q, da, wq = query_projections(own, g, weights)
    even_2, q = together((even_2, q))
    even_3, odd_3 = exchange(odd_2, even_2)
    kv2 = halo_projections(parity, even_2, odd_2, wk, wv)
    kvs = [kv0, kv1, kv2, halo_projections(parity, even_3, odd_3, wk, wv)]
    kvs = kvs[::-1]
    o, scaled, exps = attention_forward(place, key_valid.reshape(64, 2, BLOCK), q, da, kvs)

    kept, sent = outer_products(o, g, core)
    other = lax.ppermute(sent, "dp", CORE_PAIRS)
    other, *grads = together((other, *attention_backward(0, q, kvs, o, scaled, exps)))
    exps, pieces = together((exps, halve_core(place, kept, other)))
    part = send_pieces(0, pieces)
    dq, d3, d2, d1, d0 = attention_backward(1, q, kvs, o, scaled, exps, grads)
    state = back_projections(parity, d3, wk, wv)

    moved = exchange(*state)
    pieces = halve(0, place, pieces, part, state)
    terms, later = back_projections(parity, d2, wk, wv), back_projections(parity, d1, wk, wv)
    pieces = halve(1, place, pieces, send_pieces(1, pieces), (*terms, *later))
    pieces = halve(2, place, pieces, send_pieces(2, pieces))
    even, odd = moved
    odd, pieces, d0 = together((odd, pieces, d0))
    moved = exchange(hop_back(terms[0], odd), hop_back(terms[1], even))
    last = last_projections(parity, d0, dq, wq, wk, wv)
    (plane_sum,) = halve(3, place, pieces, send_pieces(3, pieces), last)
    even, odd = moved
    odd, plane_sum = together((odd, plane_sum))
    moved = exchange(hop_back(later[0], odd), hop_back(later[1], even))
    grad_tokens = final_hop(parity, last, moved)
    w_grad = sum_over_line(plane_sum, grad_tokens)
    return grad_tokens.reshape(tokens.shape), w_grad


def solution(mesh):
    placed = (
        P("dp", "blk", None, None, None),
        P("dp", None, None, None),
        P(),
        P("dp", "blk", None, None, None),
    )
    return jax.shard_map(
        per_device,
        mesh=mesh,
        in_specs=placed,
        out_specs=(P("dp", "blk", None, None, None), P("blk", "dp")),
        check_vma=False,
    )
```

```python
import jax
import jax.numpy as jnp
import numpy as np
from jax import lax
from jax.experimental import pallas as pl
from jax.experimental.pallas import tpu as pltpu
from jax.sharding import PartitionSpec as P

HEADS = 16
HEAD_DIM = 64
WIN = 4
BLOCK = 128
D = 1024
PAIR = 2 * HEAD_DIM
PAIRS_A_STEP = 4
TILE = 256
BF = jnp.bfloat16
F32 = jnp.float32

BARRED = -1e30
FREE = 3e38
SCALE = HEAD_DIM**-0.5
EXP2_SCALE = float(SCALE * np.log2(np.e))

NN = (((1,), (0,)), ((), ()))
NT = (((1,), (1,)), ((), ()))


def mm(a, b, dims=NN):
    return lax.dot_general(a, b, dims, preferred_element_type=F32)


def params(mib):
    return pltpu.CompilerParams(vmem_limit_bytes=mib * 2**20)


def cost(flops, moved, exps=0):
    return pl.CostEstimate(flops=flops // 16, bytes_accessed=moved // 16, transcendentals=exps // 16)


def in_hbm(*arrays):
    return [pltpu.with_memory_space_constraint(a, pltpu.HBM) for a in arrays]


def in_vmem(*arrays):
    return [pltpu.with_memory_space_constraint(a, pltpu.VMEM) for a in arrays]


def weight_cols(which):
    return pl.BlockSpec((D, TILE), lambda t, *_: (which, t))


def weight_rows(which):
    return pl.BlockSpec((TILE, D), lambda t, *_: (which * (D // TILE) + t, 0))


def whole(shape):
    return pl.BlockSpec(shape, lambda t, *_: (0,) * len(shape))


EVEN_PAIRS = [(i, i ^ 1) for i in range(64)]
ODD_PAIRS = [(i, i if i in (0, 63) else ((i + 1) ^ 1) - 1) for i in range(64)]


def exchange(even, odd):
    return lax.ppermute(even, "blk", EVEN_PAIRS), lax.ppermute(odd, "blk", ODD_PAIRS)


def with_parity(kernel, parity, arrays, grid, in_specs, out_specs, out_shape, mib, estimate):
    return pl.pallas_call(
        kernel,
        grid_spec=pltpu.PrefetchScalarGridSpec(
            num_scalar_prefetch=1, grid=grid, in_specs=in_specs, out_specs=out_specs
        ),
        out_shape=out_shape,
        compiler_params=params(mib),
        cost_estimate=estimate,
        name=kernel.__name__,
    )(parity, *arrays)


def halves_of(parity):
    return pl.ds(1 - parity[0], 1), pl.ds(parity[0], 1)


def first_arrays(parity, half_a, half_b, even_ref, odd_ref):
    even_ref[...] = half_a[0]
    odd_ref[...] = half_b[0]


def first_exchange(parity, x):
    shape = (1, BLOCK, D // 2)
    spec = pl.BlockSpec((BLOCK, D // 2), lambda t, p: (0, t))
    return with_parity(
        first_arrays, parity, in_hbm(x, x), (2,),
        [pl.BlockSpec(shape, lambda t, p: (p[0], 0, t)), pl.BlockSpec(shape, lambda t, p: (1 - p[0], 0, t))],
        [spec] * 2, [jax.ShapeDtypeStruct((BLOCK, D), BF)] * 2, 6, cost(0, 8 * BLOCK * D),
    )


def own_kernel(x_ref, wk_ref, wv_ref, kv_ref, wk_out, wv_out):
    wk_out[...] = wk_ref[...]
    wv_out[...] = wv_ref[...]
    x = x_ref[...].reshape(2 * BLOCK, D)
    kv_ref[0] = mm(x, wk_ref[...]).astype(BF).reshape(2, BLOCK, TILE)
    kv_ref[1] = mm(x, wv_ref[...]).astype(BF).reshape(2, BLOCK, TILE)


def own_projections(x, weights):
    return pl.pallas_call(
        own_kernel,
        grid=(D // TILE,),
        in_specs=[whole((2, BLOCK, D)), weight_cols(1), weight_cols(2)],
        out_specs=[pl.BlockSpec((2, 2, BLOCK, TILE), lambda t: (0, 0, 0, t))] + [weight_cols(0)] * 2,
        out_shape=[jax.ShapeDtypeStruct((2, 2, BLOCK, D), BF)] + [jax.ShapeDtypeStruct((D, D), BF)] * 2,
        compiler_params=params(12),
        cost_estimate=cost(8 * 2 * BLOCK * D * D, 12 * D * D + 12 * BLOCK * D),
        name="own_projections",
    )(*in_hbm(x, weights, weights))


def query_kernel(x_ref, g_ref, wq_ref, wo_ref, q_ref, da_ref, wq_out):
    wq_out[...] = wq_ref[...]
    x = x_ref[...].reshape(2 * BLOCK, D)
    g = g_ref[...].reshape(2 * BLOCK, D)
    q_ref[...] = mm(x, wq_ref[...]).astype(BF).reshape(2, BLOCK, TILE)
    da_ref[...] = mm(g, wo_ref[...], NT).astype(BF).reshape(2, BLOCK, TILE)


def query_projections(x, g, weights):
    rows = jax.ShapeDtypeStruct((2, BLOCK, D), BF)
    row_tile = pl.BlockSpec((2, BLOCK, TILE), lambda t: (0, 0, t))
    return pl.pallas_call(
        query_kernel,
        grid=(D // TILE,),
        in_specs=[whole((2, BLOCK, D)), whole((2, BLOCK, D)), weight_cols(0), weight_rows(3)],
        out_specs=[row_tile, row_tile, weight_cols(0)],
        out_shape=[rows, rows, jax.ShapeDtypeStruct((D, D), BF)],
        compiler_params=params(12),
        cost_estimate=cost(8 * 2 * BLOCK * D * D, 12 * D * D + 12 * BLOCK * D),
        name="query_projections",
    )(*in_hbm(x, g, weights, weights))


def halo_projections_kernel(parity, even_ref, odd_ref, wk_ref, wv_ref, kv_ref):
    x = jnp.concatenate([even_ref[...], odd_ref[...]], axis=0)
    for which, w_ref in enumerate((wk_ref, wv_ref)):
        rows = mm(x, w_ref[...]).astype(BF).reshape(2, BLOCK, TILE)
        for i, half in enumerate(halves_of(parity)):
            kv_ref[which, half] = rows[i : i + 1]


def halo_projections(parity, even, odd, wk, wv):
    return with_parity(
        halo_projections_kernel, parity, [even, odd, *in_vmem(wk, wv)], (D // TILE,),
        [whole((BLOCK, D)), whole((BLOCK, D)), weight_cols(0), weight_cols(0)],
        pl.BlockSpec((2, 2, BLOCK, TILE), lambda t, p: (0, 0, 0, t)),
        jax.ShapeDtypeStruct((2, 2, BLOCK, D), BF), 10,
        cost(4 * 2 * BLOCK * D * D, 4 * D * D + 12 * BLOCK * D),
    )


LANES = [slice(i * PAIR, (i + 1) * PAIR) for i in range(PAIRS_A_STEP)]


def first_head():
    return lax.broadcasted_iota(jnp.int32, (BLOCK, PAIR), 1) < HEAD_DIM


def split(rows):
    zero = jnp.zeros_like(rows)
    return jnp.concatenate([jnp.where(first_head(), rows, zero), jnp.where(first_head(), zero, rows)], axis=0)


def merge(rows):
    return jnp.where(first_head(), rows[:BLOCK], rows[BLOCK:])


def stacked(refs, which):
    return [jnp.concatenate([ref[which, 0, :, c] for ref in refs], axis=0) for c in LANES]


def score_limits(block, valid_ref):
    limits = []
    for back in range(WIN - 1, -1, -1):
        key_block = block - back
        slot = jnp.maximum(jnp.where(key_block < 64, key_block, 127 - key_block), 0)
        halves = valid_ref[pl.ds(slot, 1)].reshape(2, BLOCK)
        serves = jnp.where(key_block < 64, halves[:1], halves[1:])
        limit = jnp.where((serves == 1) & (key_block >= 0), FREE, BARRED)
        limits.append(jnp.broadcast_to(limit, (BLOCK, BLOCK)))
    row = lax.broadcasted_iota(jnp.int32, (BLOCK, BLOCK), 0)
    column = lax.broadcasted_iota(jnp.int32, (BLOCK, BLOCK), 1)
    limits[-1] = jnp.where(row == column, FREE, jnp.where(row > column, limits[-1], BARRED))
    bias = jnp.concatenate(limits, axis=1)
    return jnp.concatenate([bias, bias], axis=0)


def attention_out(
    place, valid_ref, q_ref, da_ref, kv3_ref, kv2_ref, kv1_ref, kv0_ref, out_ref, scaled_ref, terms_ref
):
    refs = (kv3_ref, kv2_ref, kv1_ref, kv0_ref)
    bias = score_limits(jnp.where(pl.program_id(0) == 0, place[0], 127 - place[0]), valid_ref)
    ones = jnp.ones((WIN * BLOCK, PAIR), BF)
    keys, values = stacked(refs, 0), stacked(refs, 1)
    scores = [mm(split(q_ref[0, :, c]), k, NT) for c, k in zip(LANES, keys)]
    scores = [jnp.minimum(s, bias) for s in scores]
    tops = [jnp.max(s, axis=1, keepdims=True) for s in scores]
    terms = [jnp.exp2((s - t) * EXP2_SCALE).astype(BF) for s, t in zip(scores, tops)]
    sums = [mm(t, jnp.concatenate([v, ones], axis=1)) for t, v in zip(terms, values)]
    shares = [1.0 / merge(s[:, PAIR:]) for s in sums]
    for i, c in enumerate(LANES):
        out_ref[0, :, c] = (merge(sums[i][:, :PAIR]) * shares[i]).astype(BF)
        scaled_ref[0, :, c] = (da_ref[0, :, c].astype(F32) * shares[i]).astype(BF)
        terms_ref[0, i] = terms[i]


def attention_grads(
    q_ref, kv3_ref, kv2_ref, kv1_ref, kv0_ref, out_ref, scaled_ref, terms_ref,
    dq_ref, d3_ref, d2_ref, d1_ref, d0_ref,
):
    refs = (kv3_ref, kv2_ref, kv1_ref, kv0_ref)
    keys, values = stacked(refs, 0), stacked(refs, 1)
    queries = [split(q_ref[0, :, c]) for c in LANES]
    scaled = [scaled_ref[0, :, c] for c in LANES]
    d_attn = [split(d) for d in scaled]
    terms = [terms_ref[0, i] for i in range(PAIRS_A_STEP)]
    d_probs = [mm(d, v, NT) for d, v in zip(d_attn, values)]
    deltas = [
        jnp.sum(split(d.astype(F32) * out_ref[0, :, c].astype(F32)), axis=1, keepdims=True)
        for c, d in zip(LANES, scaled)
    ]
    d_scores = [(p - d).astype(BF) * t for p, d, t in zip(d_probs, deltas, terms)]
    d_values = [mm(d.T, t).astype(BF).T for d, t in zip(d_attn, terms)]
    d_queries = [merge(mm(d, k)) for d, k in zip(d_scores, keys)]
    for c, d in zip(LANES, d_queries):
        dq_ref[0, :, c] = (d * SCALE).astype(BF)
    d_keys = [(mm(q.T, d) * SCALE).astype(BF).T for q, d in zip(queries, d_scores)]
    for c, dk, dv in zip(LANES, d_keys, d_values):
        for i, ref in enumerate((d3_ref, d2_ref, d1_ref, d0_ref)):
            ref[0, 0, :, c] = dk[i * BLOCK : (i + 1) * BLOCK]
            ref[1, 0, :, c] = dv[i * BLOCK : (i + 1) * BLOCK]


WIDTH = PAIRS_A_STEP * PAIR
ROWS = pl.BlockSpec((1, BLOCK, WIDTH), lambda h, p, *_: (h, 0, p))
PAIRED = pl.BlockSpec((2, 1, BLOCK, WIDTH), lambda h, p, *_: (0, h, 0, p))
VALID = pl.BlockSpec((64, 2, BLOCK), lambda h, p, *_: (0, 0, 0))
TERMS = pl.BlockSpec((1, PAIRS_A_STEP, 2 * BLOCK, WIN * BLOCK), lambda h, p, *_: (h, p, 0, 0))
ROWS_LOW = jax.ShapeDtypeStruct((2, BLOCK, D), BF)
PAIRED_LOW = jax.ShapeDtypeStruct((2, 2, BLOCK, D), BF)
TERMS_LOW = jax.ShapeDtypeStruct((2, HEADS // 2, 2 * BLOCK, WIN * BLOCK), BF)


def attention_forward(place, key_valid, q, da, kvs):
    return with_parity(
        attention_out, place, [key_valid, *in_vmem(q, da, *kvs)], (2, D // WIDTH),
        [VALID, ROWS, ROWS] + [PAIRED] * 4, [ROWS, ROWS, TERMS], [ROWS_LOW, ROWS_LOW, TERMS_LOW], 24,
        cost(2 * 4 * BLOCK * WIN * BLOCK * D * 2, 10 * 2**20, 2**21),
    )


def attention_backward(half, q, kvs, out, scaled, terms, so_far=()):
    rows = pl.BlockSpec((1, BLOCK, WIDTH), lambda p: (half, 0, p))
    paired = pl.BlockSpec((2, 1, BLOCK, WIDTH), lambda p: (0, half, 0, p))
    held = pl.BlockSpec((1, PAIRS_A_STEP, 2 * BLOCK, WIN * BLOCK), lambda p: (half, p, 0, 0))

    def kernel(*refs):
        attention_grads(*refs[:8], *refs[8 + len(so_far) :])

    return pl.pallas_call(
        kernel,
        grid=(D // WIDTH,),
        in_specs=[rows] + [paired] * 4 + [rows, rows, held] + [pl.BlockSpec(memory_space=pl.ANY)] * len(so_far),
        out_specs=[rows] + [paired] * 4,
        out_shape=[ROWS_LOW] + [PAIRED_LOW] * 4,
        input_output_aliases={8 + i: i for i in range(len(so_far))},
        compiler_params=params(24),
        cost_estimate=cost(6 * BLOCK * WIN * BLOCK * D * 2, 6 * 2**20),
        name="attention_grads",
    )(*in_vmem(q, *kvs, out, scaled, terms), *so_far)


def in_order(parity, ref, *lead):
    return jnp.concatenate([ref[(*lead, half)] for half in halves_of(parity)], axis=0).reshape(2 * BLOCK, D)


def back_projections_kernel(parity, d_ref, wk_ref, wv_ref, even_ref, odd_ref):
    rows = mm(in_order(parity, d_ref, 0), wk_ref[...], NT)
    rows += mm(in_order(parity, d_ref, 1), wv_ref[...], NT)
    even_ref[...] = rows[:BLOCK].astype(BF)
    odd_ref[...] = rows[BLOCK:].astype(BF)


def last_projections_kernel(parity, d_ref, dq_ref, wq_ref, wk_ref, wv_ref, even_ref, odd_ref):
    rows = mm(in_order(parity, dq_ref), wq_ref[...], NT)
    rows += mm(in_order(parity, d_ref, 0), wk_ref[...], NT)
    rows += mm(in_order(parity, d_ref, 1), wv_ref[...], NT)
    even_ref[...] = rows[:BLOCK]
    odd_ref[...] = rows[BLOCK:]


def back_projections(parity, d, wk, wv):
    return with_parity(
        back_projections_kernel, parity, in_vmem(d, wk, wv), (D // TILE,),
        [whole((2, 2, BLOCK, D)), weight_rows(0), weight_rows(0)],
        [pl.BlockSpec((BLOCK, TILE), lambda t, p: (0, t))] * 2,
        [jax.ShapeDtypeStruct((BLOCK, D), BF)] * 2, 10,
        cost(4 * 2 * BLOCK * D * D, 4 * D * D + 12 * BLOCK * D),
    )


def last_projections(parity, d, dq, wq, wk, wv):
    return with_parity(
        last_projections_kernel, parity, in_vmem(d, dq, wq, wk, wv), (D // TILE,),
        [whole((2, 2, BLOCK, D)), whole((2, BLOCK, D)), weight_rows(0), weight_rows(0), weight_rows(0)],
        [pl.BlockSpec((BLOCK, TILE), lambda t, p: (0, t))] * 2,
        [jax.ShapeDtypeStruct((BLOCK, D), F32)] * 2, 12,
        cost(6 * 2 * BLOCK * D * D, 6 * D * D + 16 * BLOCK * D),
    )


def outer_kernel(core_ref, o_ref, keep_ref, send_ref, kept_ref, sent_ref):
    o_t = o_ref[...].reshape(2 * BLOCK, D).T
    for g_ref, r_ref in ((send_ref, sent_ref), (keep_ref, kept_ref)):
        r_ref[0] = mm(o_t, g_ref[...].reshape(2 * BLOCK, TILE)).astype(BF)


def outer_products(o, g, core):
    result = jax.ShapeDtypeStruct((2, D, TILE), BF)
    result_spec = pl.BlockSpec((1, D, TILE), lambda y, c: (y, 0, 0))
    return pl.pallas_call(
        outer_kernel,
        grid_spec=pltpu.PrefetchScalarGridSpec(
            num_scalar_prefetch=1,
            grid=(2,),
            in_specs=[
                pl.BlockSpec((2, BLOCK, D), lambda y, c: (0, 0, 0)),
                pl.BlockSpec((2, BLOCK, TILE), lambda y, c: (0, 0, 2 * y + c[0])),
                pl.BlockSpec((2, BLOCK, TILE), lambda y, c: (0, 0, 2 * y + 1 - c[0])),
            ],
            out_specs=[result_spec, result_spec],
        ),
        out_shape=[result, result],
        compiler_params=params(12),
        cost_estimate=cost(4 * BLOCK * D * D, 2 * D * D + 8 * BLOCK * D),
        name="outer_products",
    )(core, *in_vmem(o, g, g))


def hop_sums(even_ref, odd_ref, from_even, from_odd):
    return (
        (even_ref[...].astype(F32) + from_odd[...].astype(F32)).astype(BF),
        (odd_ref[...].astype(F32) + from_even[...].astype(F32)).astype(BF),
    )


def hop_kernel(term_ref, moved_ref, out_ref):
    out_ref[...] = (term_ref[...].astype(F32) + moved_ref[...].astype(F32)).astype(BF)


def final_kernel(parity, even_ref, odd_ref, from_even, from_odd, out_ref):
    for half, rows in zip(halves_of(parity), hop_sums(even_ref, odd_ref, from_even, from_odd)):
        out_ref[half] = rows[None]


def hop_back(term, moved):
    spec = pl.BlockSpec((BLOCK, D // 2), lambda t: (0, t))
    return pl.pallas_call(
        hop_kernel,
        grid=(2,),
        in_specs=[spec] * 2,
        out_specs=spec,
        out_shape=jax.ShapeDtypeStruct((BLOCK, D), BF),
        compiler_params=params(6),
        cost_estimate=cost(4 * BLOCK * D, 6 * BLOCK * D),
        name="hop_back",
    )(*in_vmem(term, moved))


def final_hop(parity, terms, moved):
    spec = pl.BlockSpec((BLOCK, D // 2), lambda t, p: (0, t))
    return with_parity(
        final_kernel, parity, in_vmem(*terms, *moved), (2,), [spec] * 4,
        pl.BlockSpec((2, BLOCK, D // 2), lambda t, p: (0, 0, t)),
        jax.ShapeDtypeStruct((2, BLOCK, D), BF), 6, cost(8 * BLOCK * D, 14 * BLOCK * D),
    )


def chip(y, x, z, core):
    return ((y % 2) * 32 + x * 8 + z) * 4 + (y // 2) * 2 + core


CORE_PAIRS = [(i, i ^ 1) for i in range(4)]
LINES = [[32 * y + 8 * x + z for z in range(8)] for y in range(2) for x in range(4)]
FLIP = ((1, 0, 3, 2), (3, 2, 1, 0))


def halving_pairs(second, turn):
    pairs = []
    for y in range(4):
        for x in range(4):
            for z in range(8):
                for core in range(2):
                    along_x = (core == 0) != second
                    to = (y, FLIP[turn][x]) if along_x else (FLIP[turn][y], x)
                    pairs.append((chip(y, x, z, core), chip(*to, z, core)))
    return pairs


SHARE = 128


def places(position, shot):
    def ring(i):
        outer = (i == 0) | (i == 3)
        keep = [jnp.where(outer, 0, 1), jnp.where(outer, 3, 2)]
        send = [jnp.where(outer, 1, 0), jnp.where(outer, 2, 3)]
        return keep + send + [i // 2, 1 - i // 2]

    core = shot % 2
    x = (position // 8) % 4
    y = (shot // 2) * 2 + position // 32
    first, second = jnp.where(core == 0, x, y), jnp.where(core == 0, y, x)
    return jnp.stack([position, core] + ring(first) + ring(second)).astype(jnp.int32)


FIRST, SECOND = 2, 8


def total(a, b):
    return (a.astype(F32) + b.astype(F32)).astype(BF)


def split_core(place, kept_ref, other_ref, keep_ref, send_ref):
    for out_ref, at in ((keep_ref, FIRST), (send_ref, FIRST + 2)):
        for i in range(2):
            for j in range(4):
                first = place[at + i]
                y = pl.ds(jnp.where(place[1] == 0, j, first), 1)
                x = pl.ds(jnp.where(place[1] == 0, first, j), 1)
                out_ref[i : i + 1, j : j + 1] = total(kept_ref[y, x], other_ref[y, x])


def split_first(place, kept_ref, moved_ref, keep_ref, send_ref):
    for j, out_ref in enumerate((keep_ref, send_ref)):
        i = pl.ds(place[FIRST + 4 + j], 1)
        out_ref[...] = total(kept_ref[i], moved_ref[i])


def split_second(place, kept_ref, moved_ref, keep_ref, send_ref):
    for out_ref, at in ((keep_ref, SECOND), (send_ref, SECOND + 2)):
        for j in range(2):
            i = pl.ds(place[at + j], 1)
            out_ref[:, j : j + 1] = total(kept_ref[:, i], moved_ref[:, i])


def split_third(place, kept_ref, moved_ref, keep_ref, send_ref):
    for j, out_ref in enumerate((keep_ref, send_ref)):
        i = pl.ds(place[SECOND + 4 + j], 1)
        out_ref[...] = total(kept_ref[:, i], moved_ref[:, i])


def join_last(place, kept_ref, moved_ref, out_ref):
    out_ref[...] = total(kept_ref[...], moved_ref[...])


def halving(kernel, place, arrays, shapes, ready=()):
    vmem = pl.BlockSpec(memory_space=pltpu.VMEM)
    count = 1 + len(arrays)

    def body(*refs):
        kernel(*refs[:count], *refs[count + len(ready) :])

    return pl.pallas_call(
        body,
        in_specs=[pl.BlockSpec(memory_space=pltpu.SMEM)]
        + [vmem] * len(arrays)
        + [pl.BlockSpec(memory_space=pl.ANY)] * len(ready),
        out_specs=[vmem] * len(shapes),
        out_shape=[jax.ShapeDtypeStruct(shape + (SHARE, TILE), BF) for shape in shapes],
        compiler_params=params(8),
        cost_estimate=cost(2**20, 2**20),
        name=kernel.__name__,
    )(place, *arrays, *ready)


def halve_core(place, kept, other):
    arrays = [v.reshape(4, 4, SHARE, TILE) for v in (kept, other)]
    return halving(split_core, place, arrays, [(2, 4)] * 2)


HALVINGS = (
    (split_first, halving_pairs(False, 0), [(1, 4)] * 2),
    (split_second, halving_pairs(False, 1), [(1, 2)] * 2),
    (split_third, halving_pairs(True, 0), [(1, 1)] * 2),
    (join_last, halving_pairs(True, 1), [(1, 1)]),
)


together = lax.optimization_barrier


def send_pieces(turn, pieces):
    return lax.ppermute(pieces[1], ("blk", "dp"), HALVINGS[turn][1])


def halve(turn, place, pieces, moved, ready=()):
    kernel, _, shapes = HALVINGS[turn]
    return halving(kernel, place, [pieces[0], moved], shapes, ready)


def sum_over_line(total, ready):
    total = lax.all_to_all(total.reshape(8, 16, TILE), "blk", 0, 0, axis_index_groups=LINES)
    return jnp.sum(together((total, ready))[0].astype(F32), axis=0)


def per_device(tokens, key_valid, weights, out_grad):
    position = lax.axis_index("blk")
    shot = lax.axis_index("dp")
    x = tokens.reshape(2, BLOCK, D)
    g = out_grad.reshape(2, BLOCK, D)

    parity = (position % 2).reshape(1)
    state = first_exchange(parity, x)
    core = (shot % 2).reshape(1)
    place = places(position, shot)
    own, core, place = lax.optimization_barrier((x, core, place))
    kv0, wk, wv = own_projections(own, weights)
    even, odd = exchange(*state)
    even, kv0 = together((even, kv0))
    even_2, odd_2 = exchange(odd, even)
    kv1 = halo_projections(parity, even, odd, wk, wv)
    q, da, wq = query_projections(own, g, weights)
    even_2, q = together((even_2, q))
    even_3, odd_3 = exchange(odd_2, even_2)
    kv2 = halo_projections(parity, even_2, odd_2, wk, wv)
    kvs = [kv0, kv1, kv2, halo_projections(parity, even_3, odd_3, wk, wv)]
    kvs = kvs[::-1]
    o, scaled, exps = attention_forward(place, key_valid.reshape(64, 2, BLOCK), q, da, kvs)

    kept, sent = outer_products(o, g, core)
    other = lax.ppermute(sent, "dp", CORE_PAIRS)
    other, *grads = together((other, *attention_backward(0, q, kvs, o, scaled, exps)))
    exps, pieces = together((exps, halve_core(place, kept, other)))
    part = send_pieces(0, pieces)
    dq, d3, d2, d1, d0 = attention_backward(1, q, kvs, o, scaled, exps, grads)
    state = back_projections(parity, d3, wk, wv)

    moved = exchange(*state)
    pieces = halve(0, place, pieces, part, state)
    terms, later = back_projections(parity, d2, wk, wv), back_projections(parity, d1, wk, wv)
    pieces = halve(1, place, pieces, send_pieces(1, pieces), (*terms, *later))
    pieces = halve(2, place, pieces, send_pieces(2, pieces))
    even, odd = moved
    odd, pieces, d0 = together((odd, pieces, d0))
    moved = exchange(hop_back(terms[0], odd), hop_back(terms[1], even))
    last = last_projections(parity, d0, dq, wq, wk, wv)
    (plane_sum,) = halve(3, place, pieces, send_pieces(3, pieces), last)
    even, odd = moved
    moved = exchange(hop_back(later[0], odd), hop_back(later[1], even))
    grad_tokens = final_hop(parity, last, moved)
    w_grad = sum_over_line(plane_sum, grad_tokens)
    return grad_tokens.reshape(tokens.shape), w_grad


def solution(mesh):
    placed = (
        P("dp", "blk", None, None, None),
        P("dp", None, None, None),
        P(),
        P("dp", "blk", None, None, None),
    )
    return jax.shard_map(
        per_device,
        mesh=mesh,
        in_specs=placed,
        out_specs=(P("dp", "blk", None, None, None), P("blk", "dp")),
        check_vma=False,
    )
```
